512 devices in a mesh: exp: 4 (over x), patch: 128 (over z, y, core).
Axes of the slice: x: 4, y: 8, z: 8, core: 2. Of those that a mesh axis runs over, the one named last changes fastest.
Arguments:
- science_flux: float32 [4, 256, 128, 128], P('exp', 'patch'), may hold values from -6 to 6
- science_var: float32 [4, 256, 128, 128], P('exp', 'patch'), may hold values from 0.5 to 2
- templ_flux: float32 [128, 4, 150, 150], P('patch', 'exp'), may hold values from -6 to 6
- templ_var: float32 [128, 4, 150, 150], P('patch', 'exp'), may hold values from 0.5 to 2
- kernel_coefs: float32 [4, 189, 192], P('exp'), may hold values from -3 to 3
- tile_route: int32 [4, 256, 5], P('exp', 'patch'), may hold values from 0 to 188, as said below
Outputs:
- difference: float32 [4, 256, 2, 128, 128], P('exp', 'patch')
The draws below stay inside these ranges and needn't reach their ends.
Inputs may be any that keep to these rules, and one draw needn't show every extreme that they name: `tile_route`: column 0 lies in 0..4, column 1 in 0..3, columns 2 and 3 in 0..31, column 4 in 0..188. Among the 2 tiles of one exposure on one patch device at most 1 have the same column 0, and some value of column 0 is taken by exactly 1 of them.
All inputs are finite; a program needn't handle non-finite values.
Results may differ from the reference program's by a relative error of at most 0.0003.
Values sent between devices are 32-bit elements; how exact they have to be, the bound alone decides.
A program may use at most 64 MiB of HBM per device.

```python
import math
import jax
import jax.numpy as jnp
from jax import lax

TILE_DEV = 2
TPL_DEV = 4
TILE = 128
HALF = 11
BASES = 32
TERMS = 6
DETS = 189
DET_SIDE = 32
OFFSETS = 5
CAP = 1
KSIZE = 23
PAD = 150
EXPOSURES = 4
PATCHES = 128
TILES = 256


def draw_tile_route(key, part):
    key = jax.random.fold_in(key, 7)
    blocks = EXPOSURES * TILES // TILE_DEV
    keys = jax.random.split(key, blocks)

    def one_block(block_key):
        parts_keys = jax.random.split(block_key, 7)
        star = jax.random.randint(parts_keys[0], (), 0, OFFSETS)
        others = (star + 1 + jnp.repeat(jnp.arange(OFFSETS - 1), CAP)) % OFFSETS
        others = jax.random.permutation(parts_keys[1], others)
        offsets = jnp.concatenate([jnp.full((CAP,), star, jnp.int32), others[:TILE_DEV - CAP].astype(jnp.int32)])
        offsets = jax.random.permutation(parts_keys[2], offsets)
        templ_ids = jax.random.randint(parts_keys[3], (TILE_DEV,), 0, TPL_DEV)
        rows_ids = jax.random.randint(parts_keys[4], (TILE_DEV,), 0, DET_SIDE)
        cols_ids = jax.random.randint(parts_keys[5], (TILE_DEV,), 0, DET_SIDE)
        det_ids = jax.random.randint(parts_keys[6], (TILE_DEV,), 0, DETS)
        return jnp.stack([offsets, templ_ids, rows_ids, cols_ids, det_ids], -1).astype(jnp.int32)
    return jax.vmap(one_block)(keys).reshape(EXPOSURES, TILES, 5)


def level_of(stream_key, dims, cuts, low, high):
    level = 1.0
    for position, blocks in cuts:
        heights = jax.random.uniform(jax.random.fold_in(jax.random.fold_in(stream_key, 6), position), (blocks,), jnp.float32, low / len(cuts), high / len(cuts))
        level = level * jnp.repeat(jnp.exp(heights), dims[position] // blocks).reshape((-1,) + (1,) * (len(dims) - 1 - position))
    return level


def normal_values(key, dims, spread, most, shards=(), kind=jnp.bfloat16):
    values = spread * jax.random.normal(key, dims, jnp.float32)
    if shards:
        values = values * level_of(key, dims, shards, -0.22, 0.18)
    return jnp.clip(values, -most, most).astype(kind)


def setup_inputs(seed: int = 0) -> dict:
    key_of = jax.random.split(jax.random.key(seed), 7)
    science_flux = normal_values(key_of[0], (EXPOSURES, TILES, TILE, TILE), 1.0, 6.0, ((0, 4), (1, 128)), jnp.float32)
    science_var = jnp.clip(jnp.exp(math.log(2.0) - 1.3862944 * jax.random.uniform(key_of[1], (EXPOSURES, TILES, TILE, TILE), jnp.float32) ** level_of(key_of[1], (EXPOSURES, TILES, TILE, TILE), ((0, 4), (1, 128)), -0.2, 0.2)), 0.5, 2.0)
    templ_flux = normal_values(key_of[2], (PATCHES, TPL_DEV, PAD, PAD), 1.0, 6.0, ((0, 128), (1, 4)), jnp.float32)
    templ_var = jnp.clip(jnp.exp(math.log(2.0) - 1.3862944 * jax.random.uniform(key_of[3], (PATCHES, TPL_DEV, PAD, PAD), jnp.float32) ** level_of(key_of[3], (PATCHES, TPL_DEV, PAD, PAD), ((0, 128), (1, 4)), -0.2, 0.2)), 0.5, 2.0)
    kernel_coefs = normal_values(key_of[4], (EXPOSURES, DETS, BASES * TERMS), 0.5, 3.0, ((0, 4),), jnp.float32)
    tile_route = draw_tile_route(jax.random.fold_in(key_of[6], 71), 0)
    return dict(science_flux=science_flux, science_var=science_var, templ_flux=templ_flux, templ_var=templ_var, kernel_coefs=kernel_coefs, tile_route=tile_route)


HIGH = lax.Precision.HIGHEST


def power_of(ratio, degree):
    deg = degree[:, None]
    return jnp.where(deg == 0, jnp.ones_like(ratio), jnp.where(deg == 1, ratio, jnp.where(deg == 2, ratio * ratio, ratio * ratio * ratio)))


def build_tables():
    basis_ids = jnp.arange(BASES)
    sigma = 1.5 + 1.5 * (basis_ids % 2).astype(jnp.float32)
    deg_rows = (basis_ids // 2) % 4
    deg_cols = (basis_ids // 8) % 4
    lags = (jnp.arange(KSIZE) - HALF).astype(jnp.float32)
    ratio = lags[None, :] / sigma[:, None]
    envelope = jnp.exp(-0.5 * ratio * ratio)
    prow = power_of(ratio, deg_rows) * envelope
    prow = prow / jnp.sum(jnp.abs(prow), 1, keepdims=True)
    pcol = power_of(ratio, deg_cols) * envelope
    pcol = pcol / jnp.sum(jnp.abs(pcol), 1, keepdims=True)
    big_idx = jnp.arange(PAD)[:, None, None]
    small_idx = jnp.arange(TILE)[None, :, None]
    lag_idx = jnp.arange(KSIZE)[None, None, :]
    onehot = (big_idx - small_idx == lag_idx).astype(jnp.float32)
    row_toep = jnp.einsum('bu,iyu->byi', prow, onehot, precision=HIGH).reshape(BASES * TILE, PAD)
    col_toep = jnp.einsum('bv,jxv->bjx', pcol, onehot, precision=HIGH)
    return prow, pcol, onehot, row_toep, col_toep


def poly_terms(xs, ys):
    ones = jnp.ones_like(xs * ys)
    return jnp.stack([ones, xs * ones, ys * ones, xs * xs * ones, xs * ys, ys * ys * ones])


def process(tmpl_flux, tmpl_var, sci_flux, sci_var, coef_row, row_pos, col_pos, tables):
    prow, pcol, onehot, row_toep, col_toep = tables
    first = jnp.dot(row_toep, tmpl_flux, precision=HIGH).reshape(BASES, TILE, PAD)
    conv = jnp.einsum('byj,bjx->byx', first, col_toep, precision=HIGH)
    scale = TILE * DET_SIDE * 0.5
    pixels = jnp.arange(TILE).astype(jnp.float32) + 0.5
    xs = (col_pos * TILE + pixels) / scale - 1.0
    ys = (row_pos * TILE + pixels) / scale - 1.0
    terms = poly_terms(xs[None, :], ys[:, None])
    weights = coef_row.reshape(BASES, TERMS)
    mixed = jnp.einsum('bk,byx->kyx', weights, conv, precision=HIGH)
    diff = sci_flux - jnp.sum(mixed * terms, 0)
    cen_x = (col_pos * TILE + TILE * 0.5) / scale - 1.0
    cen_y = (row_pos * TILE + TILE * 0.5) / scale - 1.0
    centre = poly_terms(cen_x, cen_y)
    centre_w = jnp.dot(weights, centre, precision=HIGH)
    kernel = jnp.einsum('b,bu,bv->uv', centre_w, prow, pcol, precision=HIGH)
    squared = kernel * kernel
    wide = jnp.einsum('uv,jxv->ujx', squared, onehot, precision=HIGH)
    shifted = jnp.stack([tmpl_var[lag:lag + TILE] for lag in range(KSIZE)])
    vconv = jnp.einsum('uyj,ujx->yx', shifted, wide, precision=HIGH)
    return diff, sci_var + vconv


def reference(science_flux, science_var, templ_flux, templ_var, kernel_coefs, tile_route):
    tables = build_tables()
    count = EXPOSURES * TILES
    flat_flux = science_flux.reshape(count, TILE, TILE)
    flat_var = science_var.reshape(count, TILE, TILE)
    flat_route = tile_route.reshape(count, 5)
    ids = jnp.arange(count).astype(jnp.int32)

    def one_tile(item):
        ident, sflux, svar, route = item
        expo = ident // TILES
        within = ident % TILES
        owner = (within // TILE_DEV + route[0] - OFFSETS // 2) % PATCHES
        tflux = templ_flux[owner, route[1]]
        tvar = templ_var[owner, route[1]]
        coef_row = kernel_coefs[expo, route[4]]
        diff, var = process(tflux, tvar, sflux, svar, coef_row, route[2].astype(jnp.float32), route[3].astype(jnp.float32), tables)
        return jnp.stack([diff, var])

    result = lax.map(one_tile, (ids, flat_flux, flat_var, flat_route))
    return result.reshape(EXPOSURES, TILES, 2, TILE, TILE)
```

```python
import functools

import jax
import jax.numpy as jnp
import ml_dtypes
import numpy as np
from jax import lax
from jax.experimental import pallas as pl
from jax.experimental.pallas import tpu as pltpu
from jax.sharding import PartitionSpec as P

TILE = 128
HALF = 11
KSIZE = 23
PAD = 150
BASES = 32
TERMS = 6
DET_SIDE = 32
COLS = BASES * TERMS
MAIN = 152
REM = PAD - TILE
PACKED = MAIN + 32
GROUPS = 5
ROWS = 160
HALF_A = 96
CENTRE = 2
SCALE = TILE * DET_SIDE * 0.5
MESH = pl.DeviceIdType.MESH
BF16 = jnp.bfloat16
F32 = jnp.float32
HIGH = lax.Precision.HIGHEST


def split_np(x):
    hi = x.astype(np.float32).astype(ml_dtypes.bfloat16)
    lo = (x - hi.astype(np.float64)).astype(ml_dtypes.bfloat16)
    return hi, lo


def make_tables():
    lags = np.arange(KSIZE) - HALF
    prof = np.zeros((8, KSIZE))
    for s in range(2):
        for m in range(4):
            ratio = lags / (1.5 + 1.5 * s)
            row = ratio**m * np.exp(-0.5 * ratio * ratio)
            prof[s * 4 + m] = row / np.abs(row).sum()
    toep = np.zeros((8, PAD, TILE))
    for u in range(KSIZE):
        for x in range(TILE):
            toep[:, x + u, x] = prof[:, u]
    cols = toep.transpose(1, 0, 2).reshape(PAD, 8 * TILE)
    hi, lo = split_np(cols)
    ca = np.zeros((4 * TILE, 8 * TILE), ml_dtypes.bfloat16)
    ca[0:128] = hi[:128]
    ca[128:256] = hi[:128]
    ca[256:384] = lo[:128]
    ca[384 : 384 + REM] = hi[128:]
    ca[416 : 416 + REM] = hi[128:]
    ca[448 : 448 + REM] = lo[128:]
    rows = np.zeros((TILE, 8, ROWS))
    rows[:, :, :PAD] = toep.transpose(2, 0, 1)
    hi, lo = split_np(rows.reshape(TILE, 8 * ROWS))
    rh = np.concatenate([hi, lo], 0)
    xdeg = [0, 1, 0, 2, 1, 0]
    ydeg = [0, 0, 1, 0, 1, 2]
    pick = np.zeros((96, COLS), np.float32)
    pick2 = np.zeros((8, COLS), np.float32)
    deg = np.zeros((COLS, TILE), np.float32)
    rev = np.zeros((COLS, TILE), np.float32)
    term = np.zeros((8, COLS), np.float32)
    for b in range(BASES):
        s, mx, my = b % 2, b // 2 % 4, b // 8 % 4
        for k in range(TERMS):
            col = b * TERMS + k
            pick[((s * 4 + mx) * 3 + ydeg[k]) * 4 + my, col] = 1
            pick2[s * 4 + mx, col] = 1
            deg[col] = xdeg[k]
            term[:, col] = k
            for v in range(KSIZE):
                rev[col, -v % TILE] = prof[s * 4 + my, v]
    prow = np.zeros((24, 8), np.float32)
    prow[:KSIZE] = prof.T
    return ca, rh, pick, pick2, deg, rev, term, prow


def exchange_kernel(route, tf, tv, sel, raw, gath, ysend, recv, rqs, rqr, ld_sem, xs, xr, ys, yr, rs, rr):
    e = lax.axis_index("exp")
    p = lax.axis_index("patch")
    ne = lax.axis_size("exp")
    npatch = lax.axis_size("patch")
    right = (lax.rem(e + 1, ne), p)
    left = (lax.rem(e + ne - 1, ne), p)

    def along(d):
        return (e, lax.rem(p + d + npatch, npatch))

    loads = [pltpu.make_async_copy(src, raw.at[c], ld_sem.at[c]) for c, src in enumerate((tf, tv))]
    for load in loads:
        load.start()
    barrier = pltpu.get_barrier_semaphore()
    others = [right, left] + [along(d) for d in (-2, -1, 1, 2)]
    for other in others:
        pl.semaphore_signal(barrier, inc=1, device_id=other, device_id_type=MESH)

    ids = []
    for k in range(5):
        want = jnp.int32(0)
        for t in range(2):
            want = jnp.where(route[t, 0] == k, route[t, 1], want)
        want = lax.rem(want - e + ne, ne)
        ids.append(want)
        rqs[k] = jnp.full((8, TILE), want, jnp.int32)

    lane = lax.broadcasted_iota(jnp.int32, (32, TILE), 1)
    for c in range(2):
        loads[c].wait()
        gath[c, 0, 0:PAD, :] = raw[c, :, 0:TILE]
        gath[c, 0, PAD:MAIN, :] = jnp.zeros((MAIN - PAD, TILE), F32)
        packed = jnp.zeros((32, TILE), F32)
        for g in range(GROUPS):
            n = min(32, PAD - 32 * g)
            part = raw[c, 32 * g : 32 * g + n, TILE:PAD]
            part = jnp.concatenate([part, jnp.zeros((n, TILE - REM), F32)], 1)
            if n < 32:
                part = jnp.concatenate([part, jnp.zeros((32 - n, TILE), F32)], 0)
            if g:
                part = pltpu.roll(part, REM * g, 1)
            packed = packed + part
        gath[c, 0, MAIN:PACKED, :] = packed

    pl.semaphore_wait(barrier, len(others))

    def copy(src, dst, ssem, rsem, to):
        return pltpu.make_async_remote_copy(
            src_ref=src, dst_ref=dst, send_sem=ssem, recv_sem=rsem, device_id=to, device_id_type=MESH
        )

    part_a = pl.ds(0, HALF_A)
    part_b = pl.ds(HALF_A, PACKED - HALF_A)
    sends = []
    asks = {}
    for d in (-2, -1, 1, 2):
        k = d + CENTRE
        asks[k] = copy(rqs.at[k], rqr.at[k], rs.at[k], rr.at[k], along(d))
        asks[k].start()
    firsts = []
    for c in range(2):
        mine = gath.at[c, 0]
        four = [
            copy(mine.at[part_a], gath.at[c, 3, part_a], xs.at[c, 0], xr.at[c, 0], right),
            copy(mine.at[part_b], gath.at[c, 1, part_b], xs.at[c, 1], xr.at[c, 1], left),
            copy(mine.at[part_b], gath.at[c, 3, part_b], xs.at[c, 2], xr.at[c, 2], right),
            copy(mine.at[part_a], gath.at[c, 1, part_a], xs.at[c, 3], xr.at[c, 3], left),
        ]
        for one in four:
            one.start()
        firsts.append(four)
    for d in (-2, -1, 1, 2):
        asks[d + CENTRE].wait()
    answers = []
    for c in range(2):
        four = firsts[c]
        relays = []
        four[0].wait_recv()
        relays.append(copy(gath.at[c, 3, part_a], gath.at[c, 2, part_a], xs.at[c, 4], xr.at[c, 4], right))
        relays[0].start()
        four[1].wait_recv()
        relays.append(copy(gath.at[c, 1, part_b], gath.at[c, 2, part_b], xs.at[c, 5], xr.at[c, 5], left))
        relays[1].start()
        four[2].wait_recv()
        four[3].wait_recv()
        relays[0].wait_recv()
        relays[1].wait_recv()
        sends += four + relays
        for k in (0, 4, 1, 3, 2):
            asked = rqr[k, 0:1, :] if k != CENTRE else rqs[k, 0:1, :]
            asked = jnp.broadcast_to(asked, (PACKED, TILE))
            value = gath[c, 3]
            for j in (2, 1, 0):
                value = jnp.where(asked == j, gath[c, j], value)
            if k == CENTRE:
                recv[c, k] = value
            else:
                ysend[c, k] = value
                answer = copy(ysend.at[c, k], recv.at[c, k], ys.at[c, k], yr.at[c, k], along(CENTRE - k))
                answer.start()
                answers.append(answer)
    for one in answers:
        one.wait_recv()
    for t in range(2):
        for c in range(2):
            sel[t, c] = recv[c, route[t, 0]]
    for one in sends + answers:
        one.wait_send()


def fill_lhs(src, dst):
    main = src[0:MAIN, :]
    main = jnp.concatenate([main, jnp.zeros((ROWS - MAIN, TILE), F32)], 0)
    hi = main.astype(BF16)
    dst[:, 0:128] = hi
    dst[:, 128:256] = (main - hi.astype(F32)).astype(BF16)
    dst[:, 256:384] = hi
    other = src[MAIN:PACKED, :]
    lane = lax.broadcasted_iota(jnp.int32, (32, TILE), 1)
    for g in range(GROUPS):
        part = pltpu.roll(other, TILE - REM * g, 1) if g else other
        part = jnp.where(lane < REM, part, 0.0)
        hi = part.astype(BF16).astype(F32)
        part = hi + pltpu.roll(part - hi, 32, 1) + pltpu.roll(hi, 64, 1)
        dst[32 * g : 32 * g + 32, 384:512] = part.astype(BF16)


def prepare(t, route, kc, pick, pick2, deg, rev, term, prow, alpha, toep):
    coefs = kc[pl.ds(route[t, 4], 1), :]
    row = route[t, 2].astype(F32)
    col = route[t, 3].astype(F32)
    lanes = lax.broadcasted_iota(jnp.int32, (1, TILE), 1).astype(F32)
    xs = (col * TILE + lanes + 0.5) / SCALE - 1.0
    powers = jnp.where(deg[...] == 0.0, 1.0, jnp.where(deg[...] == 1.0, xs, xs * xs))
    alpha[t] = jnp.dot(pick[...] * coefs, powers, precision=HIGH, preferred_element_type=F32)
    cx = (col * TILE + TILE * 0.5) / SCALE - 1.0
    cy = (row * TILE + TILE * 0.5) / SCALE - 1.0
    kinds = term[...]
    centre = jnp.where(kinds == 0.0, 1.0, 0.0)
    for k, value in enumerate((cx, cy, cx * cx, cx * cy, cy * cy)):
        centre = jnp.where(kinds == k + 1.0, value, centre)
    mixed = jnp.dot(pick2[...] * centre * coefs, rev[...], precision=HIGH, preferred_element_type=F32)
    kernel = jnp.dot(prow[...], mixed, precision=HIGH, preferred_element_type=F32)
    squared = kernel * kernel
    sub = lax.broadcasted_iota(jnp.int32, (32, TILE), 0)
    lane = lax.broadcasted_iota(jnp.int32, (32, TILE), 1)
    low = lane <= sub
    for u in range(KSIZE):
        at = ((u % 8) * 3 + u // 8) * TILE
        at = slice(at, at + TILE)
        base = jnp.broadcast_to(squared[u : u + 1, :], (TILE, TILE))
        circ = pltpu.roll(base, 0, 1, stride=1, stride_axis=0)
        top = circ[0:32]
        main = jnp.concatenate([jnp.where(low, top, 0.0), circ[32:]], 0)
        rest = jnp.where(low, 0.0, top)
        hi = main.astype(BF16)
        toep[t, 0:128, at] = hi
        toep[t, 128:256, at] = hi
        toep[t, 256:384, at] = (main - hi.astype(F32)).astype(BF16)
        hi = rest.astype(BF16)
        toep[t, 384:416, at] = hi
        toep[t, 416:448, at] = hi
        toep[t, 448:480, at] = (rest - hi.astype(F32)).astype(BF16)
        toep[t, 480:512, at] = jnp.zeros((32, TILE), BF16)


def mix_columns(t, lhs, ca, hbuf, alpha, uh, ul):
    hbuf[...] = jnp.dot(lhs[...], ca[...], preferred_element_type=F32)

    def chunk(i, carry):
        at = pl.ds(pl.multiple_of(i * 16, 16), 16)
        for s in range(2):
            parts = [hbuf[at, (s * 4 + my) * TILE : (s * 4 + my + 1) * TILE] for my in range(4)]
            for mx in range(4):
                for j in range(3):
                    first = ((s * 4 + mx) * 3 + j) * 4
                    total = alpha[t, first : first + 1, :] * parts[0]
                    for my in range(1, 4):
                        total = total + alpha[t, first + my : first + my + 1, :] * parts[my]
                    to = pl.ds(pl.multiple_of((s * 4 + mx) * ROWS + i * 16, 16), 16)
                    cols = slice((t * 3 + j) * TILE, (t * 3 + j + 1) * TILE)
                    hi = total.astype(BF16)
                    uh[to, cols] = hi
                    ul[to, cols] = (total - hi.astype(F32)).astype(BF16)
        return carry

    lax.fori_loop(0, ROWS // 16, chunk, 0)


def rows_of(t, route, z):
    row = route[t, 2].astype(F32)
    subs = lax.broadcasted_iota(jnp.int32, (TILE, TILE), 0).astype(F32)
    ys = (row * TILE + subs + 0.5) / SCALE - 1.0
    z = z[:, t * 384 : (t + 1) * 384]
    return z[:, 0:128] + ys * (z[:, 128:256] + ys * z[:, 256:384])


def variance(t, lhs, toep):
    acc = jnp.zeros((TILE, TILE), F32)
    for r in range(8):
        width = 384 if r < 7 else 256
        part = jnp.dot(lhs[...], toep[t, :, r * 384 : r * 384 + width], preferred_element_type=F32)
        total = part[0:136, 0:128] + part[8:144, 128:256]
        if width == 384:
            total = total + part[16:152, 256:384]
        acc = acc + total[r : r + TILE]
    return acc


def compute_kernel(route, sel, sf, sv, kc, ca, rh, pick, pick2, deg, rev, term, prow, out, lhs, alpha, toep, hbuf, uh, ul):
    for t in range(2):
        prepare(t, route, kc, pick, pick2, deg, rev, term, prow, alpha, toep)
    for t in range(2):
        fill_lhs(sel.at[t, 0], lhs)
        mix_columns(t, lhs, ca, hbuf, alpha, uh, ul)
    z = jnp.dot(rh[...], uh[...], preferred_element_type=F32)
    z = z[0:128] + z[128:256] + jnp.dot(rh[0:128, :], ul[...], preferred_element_type=F32)
    for t in range(2):
        out[t, 0] = sf[t] - rows_of(t, route, z)
    for t in range(2):
        fill_lhs(sel.at[t, 1], lhs)
        out[t, 1] = sv[t] + variance(t, lhs, toep)


def per_device(science_flux, science_var, templ_flux, templ_var, kernel_coefs, tile_route):
    route = tile_route[0]
    vmem = pl.BlockSpec(memory_space=pltpu.VMEM)
    smem = pl.BlockSpec(memory_space=pltpu.SMEM)
    hbm = pl.BlockSpec(memory_space=pl.ANY)
    dma = pltpu.SemaphoreType.DMA
    sel = pl.pallas_call(
        exchange_kernel,
        out_shape=jax.ShapeDtypeStruct((2, 2, PACKED, TILE), F32),
        in_specs=[smem, hbm, hbm],
        out_specs=vmem,
        scratch_shapes=[
            pltpu.VMEM((2, PAD, PAD), F32),
            pltpu.VMEM((2, 4, PACKED, TILE), F32),
            pltpu.VMEM((2, 5, PACKED, TILE), F32),
            pltpu.VMEM((2, 5, PACKED, TILE), F32),
            pltpu.VMEM((5, 8, TILE), jnp.int32),
            pltpu.VMEM((5, 8, TILE), jnp.int32),
            dma((2,)),
            dma((2, 6)),
            dma((2, 6)),
            dma((2, 5)),
            dma((2, 5)),
            dma((5,)),
            dma((5,)),
        ],
        compiler_params=pltpu.CompilerParams(
            collective_id=0, has_side_effects=True, vmem_limit_bytes=32 * 2**20
        ),
        name="exchange",
    )(route, templ_flux[0, 0], templ_var[0, 0])
    tables = [jnp.asarray(x) for x in make_tables()]
    out = pl.pallas_call(
        compute_kernel,
        out_shape=jax.ShapeDtypeStruct((2, 2, TILE, TILE), F32),
        in_specs=[smem] + [vmem] * (4 + len(tables)),
        out_specs=vmem,
        scratch_shapes=[
            pltpu.VMEM((ROWS, 512), BF16),
            pltpu.VMEM((2, 96, TILE), F32),
            pltpu.VMEM((2, 512, 24 * TILE), BF16),
            pltpu.VMEM((ROWS, 1024), F32),
            pltpu.VMEM((8 * ROWS, 768), BF16),
            pltpu.VMEM((8 * ROWS, 768), BF16),
        ],
        compiler_params=pltpu.CompilerParams(vmem_limit_bytes=48 * 2**20),
        name="convolve",
    )(route, sel, science_flux[0], science_var[0], kernel_coefs[0], *tables)
    return out[None]


def solution(mesh):
    return jax.shard_map(
        per_device,
        mesh=mesh,
        in_specs=(
            P("exp", "patch", None, None),
            P("exp", "patch", None, None),
            P("patch", "exp", None, None),
            P("patch", "exp", None, None),
            P("exp", None, None),
            P("exp", "patch", None),
        ),
        out_specs=P("exp", "patch", None, None, None),
        check_vma=False,
    )
```

```python
import jax
import jax.numpy as jnp
import ml_dtypes
import numpy as np
from jax import lax
from jax.experimental import pallas as pl
from jax.experimental.pallas import tpu as pltpu
from jax.sharding import PartitionSpec as P

TILE = 128
HALF = 11
KSIZE = 23
PAD = 150
BASES = 32
TERMS = 6
DET_SIDE = 32
COLS = BASES * TERMS
MAIN = 152
REM = PAD - TILE
PACKED = MAIN + 32
GROUPS = 5
ROWS = 160
CUTS = ((0, 96), (96, PACKED))
N_TABLES = 8
CENTRE = 2
SCALE = TILE * DET_SIDE * 0.5
MESH = pl.DeviceIdType.MESH
BF16 = jnp.bfloat16
F32 = jnp.float32
HIGH = lax.Precision.HIGHEST


def split_np(x):
    hi = x.astype(np.float32).astype(ml_dtypes.bfloat16)
    lo = (x - hi.astype(np.float64)).astype(ml_dtypes.bfloat16)
    return hi, lo


def make_tables():
    lags = np.arange(KSIZE) - HALF
    prof = np.zeros((8, KSIZE))
    for s in range(2):
        for m in range(4):
            ratio = lags / (1.5 + 1.5 * s)
            row = ratio**m * np.exp(-0.5 * ratio * ratio)
            prof[s * 4 + m] = row / np.abs(row).sum()
    toep = np.zeros((8, PAD, TILE))
    for u in range(KSIZE):
        for x in range(TILE):
            toep[:, x + u, x] = prof[:, u]
    cols = toep.transpose(1, 0, 2).reshape(PAD, 8 * TILE)
    hi, lo = split_np(cols)
    ca = np.zeros((4 * TILE, 8 * TILE), ml_dtypes.bfloat16)
    ca[0:128] = hi[:128]
    ca[128:256] = hi[:128]
    ca[256:384] = lo[:128]
    ca[384 : 384 + REM] = hi[128:]
    ca[416 : 416 + REM] = hi[128:]
    ca[448 : 448 + REM] = lo[128:]
    rows = np.zeros((TILE, 8, ROWS))
    rows[:, :, :PAD] = toep.transpose(2, 0, 1)
    hi, lo = split_np(rows.reshape(TILE, 8 * ROWS))
    rh = np.concatenate([hi, lo], 0)
    xdeg = [0, 1, 0, 2, 1, 0]
    ydeg = [0, 0, 1, 0, 1, 2]
    pick = np.zeros((96, COLS), np.float32)
    pick2 = np.zeros((8, COLS), np.float32)
    deg = np.zeros((COLS, TILE), np.float32)
    rev = np.zeros((COLS, TILE), np.float32)
    term = np.zeros((8, COLS), np.float32)
    for b in range(BASES):
        s, mx, my = b % 2, b // 2 % 4, b // 8 % 4
        for k in range(TERMS):
            col = b * TERMS + k
            pick[((s * 4 + mx) * 3 + ydeg[k]) * 4 + my, col] = 1
            pick2[s * 4 + mx, col] = 1
            deg[col] = xdeg[k]
            term[:, col] = k
            for v in range(KSIZE):
                rev[col, -v % TILE] = prof[s * 4 + my, v]
    prow = np.zeros((24, 8), np.float32)
    prow[:KSIZE] = prof.T
    return ca, rh, pick, pick2, deg, rev, term, prow


def fill_lhs(src, dst):
    main = src[0:MAIN]
    main = jnp.concatenate([main, jnp.zeros((ROWS - MAIN, TILE), F32)], 0)
    hi = main.astype(BF16)
    dst[:, 0:128] = hi
    dst[:, 128:256] = (main - hi.astype(F32)).astype(BF16)
    dst[:, 256:384] = hi
    other = src[MAIN:PACKED]
    lane = lax.broadcasted_iota(jnp.int32, (32, TILE), 1)
    for g in range(GROUPS):
        part = pltpu.roll(other, TILE - REM * g, 1) if g else other
        part = jnp.where(lane < REM, part, 0.0)
        hi = part.astype(BF16).astype(F32)
        part = hi + pltpu.roll(part - hi, 32, 1) + pltpu.roll(hi, 64, 1)
        dst[32 * g : 32 * g + 32, 384:512] = part.astype(BF16)


def prepare(t, route, kc, pick, pick2, deg, rev, term, prow, alpha, square, toep):
    coefs = kc[route[t, 4]]
    row = route[t, 2].astype(F32)
    col = route[t, 3].astype(F32)
    lanes = lax.broadcasted_iota(jnp.int32, (1, TILE), 1).astype(F32)
    xs = (col * TILE + lanes + 0.5) / SCALE - 1.0
    powers = jnp.where(deg[...] == 0.0, 1.0, jnp.where(deg[...] == 1.0, xs, xs * xs))
    alpha[t] = jnp.dot(pick[...] * coefs, powers, precision=HIGH, preferred_element_type=F32)
    cx = (col * TILE + TILE * 0.5) / SCALE - 1.0
    cy = (row * TILE + TILE * 0.5) / SCALE - 1.0
    kinds = term[...]
    centre = jnp.where(kinds == 0.0, 1.0, 0.0)
    for k, value in enumerate((cx, cy, cx * cx, cx * cy, cy * cy)):
        centre = jnp.where(kinds == k + 1.0, value, centre)
    mixed = jnp.dot(pick2[...] * centre * coefs, rev[...], precision=HIGH, preferred_element_type=F32)
    kernel = jnp.dot(prow[...], mixed, precision=HIGH, preferred_element_type=F32)
    sub = lax.broadcasted_iota(jnp.int32, (32, TILE), 0)
    lane = lax.broadcasted_iota(jnp.int32, (32, TILE), 1)
    low = lane <= sub
    square[t] = kernel * kernel

    def lag(u, carry):
        at = pl.ds(pl.multiple_of((lax.rem(u, 8) * 3 + lax.div(u, 8)) * TILE, TILE), TILE)
        base = jnp.broadcast_to(square[t, pl.ds(u, 1), :], (TILE, TILE))
        circ = pltpu.roll(base, 0, 1, stride=1, stride_axis=0)
        top = circ[0:32]
        main = jnp.concatenate([jnp.where(low, top, 0.0), circ[32:]], 0)
        rest = jnp.where(low, 0.0, top)
        hi = main.astype(BF16)
        toep[t, 0:128, at] = hi
        toep[t, 128:256, at] = hi
        toep[t, 256:384, at] = (main - hi.astype(F32)).astype(BF16)
        hi = rest.astype(BF16)
        toep[t, 384:416, at] = hi
        toep[t, 416:448, at] = hi
        toep[t, 448:480, at] = (rest - hi.astype(F32)).astype(BF16)
        toep[t, 480:512, at] = jnp.zeros((32, TILE), BF16)
        return carry

    lax.fori_loop(0, KSIZE, lag, 0)


def mix_columns(t, lhs, ca, hbuf, alpha, uh, ul):
    hbuf[...] = jnp.dot(lhs[...], ca[...], preferred_element_type=F32)

    def chunk(i, carry):
        at = pl.ds(pl.multiple_of(i * 16, 16), 16)
        for s in range(2):
            parts = [hbuf[at, (s * 4 + my) * TILE : (s * 4 + my + 1) * TILE] for my in range(4)]
            for mx in range(4):
                for j in range(3):
                    first = ((s * 4 + mx) * 3 + j) * 4
                    total = alpha[t, first : first + 1, :] * parts[0]
                    for my in range(1, 4):
                        total = total + alpha[t, first + my : first + my + 1, :] * parts[my]
                    to = pl.ds(pl.multiple_of((s * 4 + mx) * ROWS + i * 16, 16), 16)
                    cols = slice((t * 3 + j) * TILE, (t * 3 + j + 1) * TILE)
                    hi = total.astype(BF16)
                    uh[to, cols] = hi
                    ul[to, cols] = (total - hi.astype(F32)).astype(BF16)
        return carry

    lax.fori_loop(0, ROWS // 16, chunk, 0)


def rows_of(t, route, z):
    row = route[t, 2].astype(F32)
    subs = lax.broadcasted_iota(jnp.int32, (TILE, TILE), 0).astype(F32)
    ys = (row * TILE + subs + 0.5) / SCALE - 1.0
    z = z[:, t * 384 : (t + 1) * 384]
    return z[:, 0:128] + ys * (z[:, 128:256] + ys * z[:, 256:384])


def variance(t, lhs, toep):
    acc = jnp.zeros((TILE, TILE), F32)
    for r in range(8):
        width = 384 if r < 7 else 256
        part = jnp.dot(lhs[...], toep[t, :, r * 384 : r * 384 + width], preferred_element_type=F32)
        total = part[0:136, 0:128] + part[8:144, 128:256]
        if width == 384:
            total = total + part[16:152, 256:384]
        acc = acc + total[r : r + TILE]
    return acc


def fetch(refs, buffers, sem):
    copies = [pltpu.make_async_copy(src, dst, sem.at[i]) for i, (src, dst) in enumerate(zip(refs, buffers))]
    for one in copies:
        one.start()
    return copies


def pack(raw, dst):
    dst[0:PAD, :] = raw[:, 0:TILE]
    dst[PAD:MAIN, :] = jnp.zeros((MAIN - PAD, TILE), F32)
    packed = jnp.zeros((32, TILE), F32)
    for g in range(GROUPS):
        n = min(32, PAD - 32 * g)
        part = raw[32 * g : 32 * g + n, TILE:PAD]
        part = jnp.concatenate([part, jnp.zeros((n, TILE - REM), F32)], 1)
        if n < 32:
            part = jnp.concatenate([part, jnp.zeros((32 - n, TILE), F32)], 0)
        if g:
            part = pltpu.roll(part, REM * g, 1)
        packed = packed + part
    dst[MAIN:PACKED, :] = packed


def difference_kernel(*refs):
    n = N_TABLES
    tf, tv, route_in, kc_in = refs[:4]
    tables_in, out = refs[4 : 4 + n], refs[4 + n]
    raw, route, kc = refs[5 + n : 8 + n]
    tables = refs[8 + n : 8 + 2 * n]
    gath, ysend, recv_flux, recv_var, rqs, rqr, lhs, alpha, square, toep, hbuf, uh, ul = refs[8 + 2 * n : 21 + 2 * n]
    ld_sem, tab_sem, xs, xr, ys, yr, rs, rr = refs[21 + 2 * n :]
    recv = (recv_flux, recv_var)
    ca, rh, pick, pick2, deg, rev, term, prow = tables

    e = lax.axis_index("exp")
    p = lax.axis_index("patch")
    ne = lax.axis_size("exp")
    npatch = lax.axis_size("patch")
    exposures = {k: (lax.rem(e + k, ne), p) for k in (2, 1, 3)}

    def along(d):
        return (e, lax.rem(p + d + npatch, npatch))

    barrier = pltpu.get_barrier_semaphore()
    others = list(exposures.values()) + [along(d) for d in (-2, -1, 1, 2)]
    for other in others:
        pl.semaphore_signal(barrier, inc=1, device_id=other, device_id_type=MESH)
    loads = fetch((tf.at[:, 0, :], tv.at[:, 0, :], route_in, kc_in), (raw.at[0], raw.at[1], route, kc), ld_sem)
    table_loads = fetch(tables_in, tables, tab_sem)
    loads[2].wait()
    for k in range(5):
        want = jnp.int32(0)
        for t in range(2):
            want = jnp.where(route[t, 0] == k, route[t, 1], want)
        rqs[k] = jnp.full((8, TILE), lax.rem(want - e + ne, ne), jnp.int32)
    for c in range(2):
        loads[c].wait()
        pack(raw.at[c], gath.at[c, 0])
    pl.semaphore_wait(barrier, len(others))

    def copy(src, dst, ssem, rsem, to):
        return pltpu.make_async_remote_copy(
            src_ref=src, dst_ref=dst, send_sem=ssem, recv_sem=rsem, device_id=to, device_id_type=MESH
        )

    chunks = [(c, lo, hi) for c in range(2) for lo, hi in CUTS]
    gathers, answers, asks = [], [], []
    for i, (c, lo, hi) in enumerate(chunks):
        at = pl.ds(lo, hi - lo)
        group = [
            copy(gath.at[c, 0, at], gath.at[c, 4 - k, at], xs.at[i, k], xr.at[i, k], to) for k, to in exposures.items()
        ]
        for one in group:
            one.start()
        gathers.append(group)
        if i == 0:
            for d in (-2, -1, 1, 2):
                k = d + CENTRE
                asks.append(copy(rqs.at[k], rqr.at[k], rs.at[k], rr.at[k], along(d)))
                asks[-1].start()

    def chosen(k, c, lo, hi):
        asked = rqr[k, 0:1, :] if k != CENTRE else rqs[k, 0:1, :]
        asked = jnp.broadcast_to(asked, (hi - lo, TILE))
        value = gath[c, 3, lo:hi]
        for j in (2, 1, 0):
            value = jnp.where(asked == j, gath[c, j, lo:hi], value)
        return value

    def answer(i):
        c, lo, hi = chunks[i]
        at = pl.ds(lo, hi - lo)
        for one in gathers[i]:
            one.wait_recv()
        group = []
        for k in (0, 4, 1, 3):
            ysend[c, k, lo:hi] = chosen(k, c, lo, hi)
            group.append(copy(ysend.at[c, k, at], recv[c].at[k, at], ys.at[i, k], yr.at[i, k], along(CENTRE - k)))
            group[-1].start()
        answers.append(group)

    for one in loads[3:] + table_loads:
        one.wait()
    half = len(CUTS)
    prepare(0, route, kc, pick, pick2, deg, rev, term, prow, alpha, square, toep)
    for one in asks:
        one.wait_recv()
    for i in range(half):
        answer(i)
    prepare(1, route, kc, pick, pick2, deg, rev, term, prow, alpha, square, toep)
    for i in range(half, 2 * half):
        answer(i)
    for c in range(2):
        recv[c][CENTRE] = chosen(CENTRE, c, 0, PACKED)

    for group in answers[:half]:
        for one in group:
            one.wait_recv()
    for t in range(2):
        fill_lhs(recv_flux[route[t, 0]], lhs)
        mix_columns(t, lhs, ca, hbuf, alpha, uh, ul)
    z = jnp.dot(rh[...], uh[...], preferred_element_type=F32)
    z = z[0:128] + z[128:256] + jnp.dot(rh[0:128, :], ul[...], preferred_element_type=F32)
    for t in range(2):
        out[t, 0] = -rows_of(t, route, z)
    for group in answers[half:]:
        for one in group:
            one.wait_recv()
    for t in range(2):
        fill_lhs(recv_var[route[t, 0]], lhs)
        out[t, 1] = variance(t, lhs, toep)
    for one in asks + sum(gathers, []) + sum(answers, []):
        one.wait_send()


def per_device(science_flux, science_var, templ_flux, templ_var, kernel_coefs, tile_route):
    hbm = pl.BlockSpec(memory_space=pl.ANY)
    dma = pltpu.SemaphoreType.DMA
    tables = [jnp.asarray(x) for x in make_tables()]
    n = 2 * len(CUTS)
    delta = pl.pallas_call(
        difference_kernel,
        out_shape=jax.ShapeDtypeStruct((2, 2, TILE, TILE), F32),
        in_specs=[hbm] * (4 + N_TABLES),
        out_specs=pl.BlockSpec(memory_space=pltpu.VMEM),
        scratch_shapes=[
            pltpu.VMEM((2, PAD, PAD), F32),
            pltpu.SMEM((2, 5), jnp.int32),
            pltpu.VMEM((kernel_coefs.shape[1], 1, COLS), F32),
        ]
        + [pltpu.VMEM(x.shape, x.dtype) for x in tables]
        + [
            pltpu.VMEM((2, 4, PACKED, TILE), F32),
            pltpu.VMEM((2, 5, PACKED, TILE), F32),
            pltpu.VMEM((5, PACKED, TILE), F32),
            pltpu.VMEM((5, PACKED, TILE), F32),
            pltpu.VMEM((5, 8, TILE), jnp.int32),
            pltpu.VMEM((5, 8, TILE), jnp.int32),
            pltpu.VMEM((ROWS, 512), BF16),
            pltpu.VMEM((2, 96, TILE), F32),
            pltpu.VMEM((2, 24, TILE), F32),
            pltpu.VMEM((2, 512, 24 * TILE), BF16),
            pltpu.VMEM((ROWS, 1024), F32),
            pltpu.VMEM((8 * ROWS, 768), BF16),
            pltpu.VMEM((8 * ROWS, 768), BF16),
            dma((4,)),
            dma((N_TABLES,)),
            dma((n, 4)),
            dma((n, 4)),
            dma((n, 5)),
            dma((n, 5)),
            dma((5,)),
            dma((5,)),
        ],
        compiler_params=pltpu.CompilerParams(
            collective_id=0, has_side_effects=True, vmem_limit_bytes=63 * 2**20
        ),
        name="difference",
    )(
        templ_flux[0].transpose(1, 0, 2),
        templ_var[0].transpose(1, 0, 2),
        tile_route[0],
        kernel_coefs.transpose(1, 0, 2),
        *tables,
    )
    return jnp.stack([science_flux, science_var], 2) + delta[None]


def solution(mesh):
    return jax.shard_map(
        per_device,
        mesh=mesh,
        in_specs=(
            P("exp", "patch", None, None),
            P("exp", "patch", None, None),
            P("patch", "exp", None, None),
            P("patch", "exp", None, None),
            P("exp", None, None),
            P("exp", "patch", None),
        ),
        out_specs=P("exp", "patch", None, None, None),
        check_vma=False,
    )
```

```python
import jax
import jax.numpy as jnp
import ml_dtypes
import numpy as np
from jax import lax
from jax.experimental import pallas as pl
from jax.experimental.pallas import tpu as pltpu
from jax.sharding import PartitionSpec as P

TILE = 128
HALF = 11
KSIZE = 23
PAD = 150
BASES = 32
TERMS = 6
DET_SIDE = 32
COLS = BASES * TERMS
MAIN = 152
REM = PAD - TILE
PACKED = MAIN + 32
GROUPS = 5
ROWS = 160
CUTS = ((0, 96), (96, PACKED))
N_TABLES = 8
CENTRE = 2
SCALE = TILE * DET_SIDE * 0.5
DEGREES = 6
MESH = pl.DeviceIdType.MESH
BF16 = jnp.bfloat16
F32 = jnp.float32
HIGH = lax.Precision.HIGHEST


def split_np(x):
    hi = x.astype(np.float32).astype(ml_dtypes.bfloat16)
    lo = (x - hi.astype(np.float64)).astype(ml_dtypes.bfloat16)
    return hi, lo


def power_profile(s, m):
    ratio = (np.arange(KSIZE) - HALF) / (1.5 + 1.5 * s)
    return ratio**m * np.exp(-0.5 * ratio * ratio)


def step_up(s, m):
    return (1.5 + 1.5 * s) * np.abs(power_profile(s, m + 1)).sum() / np.abs(power_profile(s, m)).sum()


def banded(profiles):
    out = np.zeros((len(profiles), PAD, TILE))
    for u in range(KSIZE):
        for x in range(TILE):
            out[:, x + u, x] = profiles[:, u]
    return out


def make_tables():
    prof = np.zeros((8, KSIZE))
    wide = np.zeros((2 * DEGREES, KSIZE))
    for s in range(2):
        for m in range(DEGREES):
            row = power_profile(s, m)
            wide[s * DEGREES + m] = row / np.abs(row).sum()
        prof[s * 4 : s * 4 + 4] = wide[s * DEGREES : s * DEGREES + 4]
    toep = banded(prof)
    cols = toep.transpose(1, 0, 2).reshape(PAD, 8 * TILE)
    hi, lo = split_np(cols)
    ca = np.zeros((4 * TILE, 8 * TILE), ml_dtypes.bfloat16)
    ca[0:128] = hi[:128]
    ca[128:256] = hi[:128]
    ca[256:384] = lo[:128]
    ca[384 : 384 + REM] = hi[128:]
    ca[416 : 416 + REM] = hi[128:]
    ca[448 : 448 + REM] = lo[128:]
    rows = np.zeros((TILE, 2 * DEGREES, ROWS))
    rows[:, :, :PAD] = banded(wide).transpose(2, 0, 1)
    hi, lo = split_np(rows.reshape(TILE, 2 * DEGREES * ROWS))
    rh = np.concatenate([hi, lo], 0)
    xdeg = [0, 1, 0, 2, 1, 0]
    ydeg = [0, 0, 1, 0, 1, 2]
    pick = np.zeros((96, COLS), np.float32)
    pick2 = np.zeros((8, COLS), np.float32)
    deg = np.zeros((COLS, TILE), np.float32)
    rev = np.zeros((COLS, TILE), np.float32)
    term = np.zeros((8, COLS), np.float32)
    for b in range(BASES):
        s, mx, my = b % 2, b // 2 % 4, b // 8 % 4
        for k in range(TERMS):
            col = b * TERMS + k
            pick[((s * 4 + mx) * 3 + ydeg[k]) * 4 + my, col] = 1
            pick2[s * 4 + mx, col] = 1
            deg[col] = xdeg[k]
            term[:, col] = k
            for v in range(KSIZE):
                rev[col, -v % TILE] = prof[s * 4 + my, v]
    prow = np.zeros((24, 8), np.float32)
    prow[:KSIZE] = prof.T
    return ca, rh, pick, pick2, deg, rev, term, prow


def fill_lhs(tiles, dst):
    lane = lax.broadcasted_iota(jnp.int32, (32, TILE), 1)
    pieces = []
    for src in tiles:
        main = jnp.concatenate([src[0:MAIN], jnp.zeros((ROWS - MAIN, TILE), F32)], 0)
        hi = main.astype(BF16)
        lo = (main - hi.astype(F32)).astype(BF16)
        other = src[MAIN:PACKED]
        parts = []
        for g in range(GROUPS):
            part = pltpu.roll(other, TILE - REM * g, 1) if g else other
            part = jnp.where(lane < REM, part, 0.0)
            top = part.astype(BF16).astype(F32)
            parts.append((top + pltpu.roll(part - top, 32, 1) + pltpu.roll(top, 64, 1)).astype(BF16))
        pieces.append((hi, lo, jnp.concatenate(parts, 0)))
    for t, (hi, lo, rest) in enumerate(pieces):
        at = slice(t * ROWS, (t + 1) * ROWS)
        dst[at, 0:128] = hi
        dst[at, 128:256] = lo
        dst[at, 256:384] = hi
        dst[at, 384:512] = rest


def prepare(t, route, kc, pick, pick2, deg, rev, term, prow, alpha, square, toep):
    coefs = kc[route[t, 4]]
    row = route[t, 2].astype(F32)
    col = route[t, 3].astype(F32)
    lanes = lax.broadcasted_iota(jnp.int32, (1, TILE), 1).astype(F32)
    xs = (col * TILE + lanes + 0.5) / SCALE - 1.0
    powers = jnp.where(deg[...] == 0.0, 1.0, jnp.where(deg[...] == 1.0, xs, xs * xs))
    alpha[t] = jnp.dot(pick[...] * coefs, powers, precision=HIGH, preferred_element_type=F32)
    cx = (col * TILE + TILE * 0.5) / SCALE - 1.0
    cy = (row * TILE + TILE * 0.5) / SCALE - 1.0
    kinds = term[...]
    centre = jnp.where(kinds == 0.0, 1.0, 0.0)
    for k, value in enumerate((cx, cy, cx * cx, cx * cy, cy * cy)):
        centre = jnp.where(kinds == k + 1.0, value, centre)
    mixed = jnp.dot(pick2[...] * centre * coefs, rev[...], precision=HIGH, preferred_element_type=F32)
    kernel = jnp.dot(prow[...], mixed, precision=HIGH, preferred_element_type=F32)
    sub = lax.broadcasted_iota(jnp.int32, (32, TILE), 0)
    lane = lax.broadcasted_iota(jnp.int32, (32, TILE), 1)
    low = lane <= sub
    square[t] = kernel * kernel

    def lag(u, carry):
        at = pl.ds(pl.multiple_of((lax.rem(u, 8) * 3 + lax.div(u, 8)) * TILE, TILE), TILE)
        base = jnp.broadcast_to(square[t, pl.ds(u, 1), :], (TILE, TILE))
        circ = pltpu.roll(base, 0, 1, stride=1, stride_axis=0)
        top = circ[0:32]
        main = jnp.concatenate([jnp.where(low, top, 0.0), circ[32:]], 0)
        rest = jnp.where(low, 0.0, top)
        hi = main.astype(BF16)
        toep[t, 0:128, at] = hi
        toep[t, 128:256, at] = hi
        toep[t, 256:384, at] = (main - hi.astype(F32)).astype(BF16)
        hi = rest.astype(BF16)
        toep[t, 384:416, at] = hi
        toep[t, 416:448, at] = hi
        toep[t, 448:480, at] = (rest - hi.astype(F32)).astype(BF16)
        toep[t, 480:512, at] = jnp.zeros((32, TILE), BF16)
        return carry

    lax.fori_loop(0, KSIZE, lag, 0)


def mix_columns(route, hbuf, alpha, uh, ul):
    def chunk(i, carry):
        subs = lax.broadcasted_iota(jnp.int32, (16, TILE), 0).astype(F32)
        for t in range(2):
            first_row = route[t, 2].astype(F32) * TILE + (i * 16).astype(F32) + (0.5 - HALF)
            yc = (subs + first_row) / SCALE - 1.0
            at = pl.ds(pl.multiple_of(t * ROWS + i * 16, 16), 16)
            for s in range(2):
                parts = [hbuf[at, (s * 4 + my) * TILE : (s * 4 + my + 1) * TILE] for my in range(4)]
                mixed = []
                for mx in range(4):
                    terms = []
                    for j in range(3):
                        first = ((s * 4 + mx) * 3 + j) * 4
                        total = alpha[t, first : first + 1, :] * parts[0]
                        for my in range(1, 4):
                            total = total + alpha[t, first + my : first + my + 1, :] * parts[my]
                        terms.append(total)
                    mixed.append(terms)
                for m in range(DEGREES):
                    total = None
                    if m < 4:
                        a, b, c = mixed[m]
                        total = a + yc * (b + yc * c)
                    if 1 <= m <= 4:
                        a, b, c = mixed[m - 1]
                        term = (b + (2.0 * yc) * c) * np.float32(-step_up(s, m - 1) / SCALE)
                        total = term if total is None else total + term
                    if m >= 2:
                        a, b, c = mixed[m - 2]
                        term = c * np.float32(step_up(s, m - 2) * step_up(s, m - 1) / SCALE**2)
                        total = term if total is None else total + term
                    to = pl.ds(pl.multiple_of((s * DEGREES + m) * ROWS + i * 16, 16), 16)
                    cols = slice(t * TILE, (t + 1) * TILE)
                    hi = total.astype(BF16)
                    uh[to, cols] = hi
                    ul[to, cols] = (total - hi.astype(F32)).astype(BF16)
        return carry

    lax.fori_loop(0, ROWS // 16, chunk, 0)


def variance(t, lhs, toep):
    acc = jnp.zeros((TILE, TILE), F32)
    for r in range(0, 8, 2):
        width = 768 if r < 6 else 640
        part = jnp.dot(
            lhs[t * ROWS : (t + 1) * ROWS, :], toep[t, :, r * 384 : r * 384 + width], preferred_element_type=F32
        )
        for k in range(2):
            at = k * 384
            total = part[0:136, at : at + 128] + part[8:144, at + 128 : at + 256]
            if at + 384 <= width:
                total = total + part[16:152, at + 256 : at + 384]
            acc = acc + total[r + k : r + k + TILE]
    return acc


def fetch(refs, buffers, sem):
    copies = [pltpu.make_async_copy(src, dst, sem.at[i]) for i, (src, dst) in enumerate(zip(refs, buffers))]
    for one in copies:
        one.start()
    return copies


def pack(raw, dst):
    dst[0:PAD, :] = raw[:, 0:TILE]
    dst[PAD:MAIN, :] = jnp.zeros((MAIN - PAD, TILE), F32)
    packed = jnp.zeros((32, TILE), F32)
    for g in range(GROUPS):
        n = min(32, PAD - 32 * g)
        part = raw[32 * g : 32 * g + n, TILE:PAD]
        part = jnp.concatenate([part, jnp.zeros((n, TILE - REM), F32)], 1)
        if n < 32:
            part = jnp.concatenate([part, jnp.zeros((32 - n, TILE), F32)], 0)
        if g:
            part = pltpu.roll(part, REM * g, 1)
        packed = packed + part
    dst[MAIN:PACKED, :] = packed


def difference_kernel(*refs):
    n = N_TABLES
    tf, tv, route_in, kc_in, sf_in, sv_in = refs[:6]
    tables_in, out = refs[6 : 6 + n], refs[6 + n]
    raw, route, kc, sci, result = refs[7 + n : 12 + n]
    tables = refs[12 + n : 12 + 2 * n]
    gath, ysend, recv_flux, recv_var, rqs, rqr, lhs, alpha, square, toep, hbuf, uh, ul = refs[12 + 2 * n : 25 + 2 * n]
    ld_sem, tab_sem, out_sem, xs, xr, ys, yr, rs, rr = refs[25 + 2 * n :]
    recv = (recv_flux, recv_var)
    ca, rh, pick, pick2, deg, rev, term, prow = tables

    e = lax.axis_index("exp")
    p = lax.axis_index("patch")
    ne = lax.axis_size("exp")
    npatch = lax.axis_size("patch")
    exposures = {k: (lax.rem(e + k, ne), p) for k in (2, 1, 3)}

    def along(d):
        return (e, lax.rem(p + d + npatch, npatch))

    barrier = pltpu.get_barrier_semaphore()
    others = list(exposures.values()) + [along(d) for d in (-2, -1, 1, 2)]
    for other in others:
        pl.semaphore_signal(barrier, inc=1, device_id=other, device_id_type=MESH)
    loads = fetch(
        (tf.at[:, 0, :], tv.at[:, 0, :], route_in, kc_in, sf_in, sv_in),
        (raw.at[0], raw.at[1], route, kc, sci.at[0], sci.at[1]),
        ld_sem,
    )
    table_loads = fetch(tables_in, tables, tab_sem)
    loads[2].wait()
    for k in range(5):
        want = jnp.int32(0)
        for t in range(2):
            want = jnp.where(route[t, 0] == k, route[t, 1], want)
        rqs[k] = jnp.full((8, TILE), lax.rem(want - e + ne, ne), jnp.int32)
    for c in range(2):
        loads[c].wait()
        pack(raw.at[c], gath.at[c, 0])
    pl.semaphore_wait(barrier, len(others))

    def copy(src, dst, ssem, rsem, to):
        return pltpu.make_async_remote_copy(
            src_ref=src, dst_ref=dst, send_sem=ssem, recv_sem=rsem, device_id=to, device_id_type=MESH
        )

    chunks = [(c, lo, hi) for c in range(2) for lo, hi in CUTS]
    gathers, answers, asks = [], [], []
    for i, (c, lo, hi) in enumerate(chunks):
        at = pl.ds(lo, hi - lo)
        group = [
            copy(gath.at[c, 0, at], gath.at[c, 4 - k, at], xs.at[i, k], xr.at[i, k], to) for k, to in exposures.items()
        ]
        for one in group:
            one.start()
        gathers.append(group)
        if i == 0:
            for d in (-2, -1, 1, 2):
                k = d + CENTRE
                asks.append(copy(rqs.at[k], rqr.at[k], rs.at[k], rr.at[k], along(d)))
                asks[-1].start()

    def chosen(k, c, lo, hi):
        asked = rqr[k, 0:1, :] if k != CENTRE else rqs[k, 0:1, :]
        asked = jnp.broadcast_to(asked, (hi - lo, TILE))
        value = gath[c, 3, lo:hi]
        for j in (2, 1, 0):
            value = jnp.where(asked == j, gath[c, j, lo:hi], value)
        return value

    def answer(i):
        c, lo, hi = chunks[i]
        at = pl.ds(lo, hi - lo)
        for one in gathers[i]:
            one.wait_recv()
        group = []
        for k in (0, 4, 1, 3):
            ysend[c, k, lo:hi] = chosen(k, c, lo, hi)
            group.append(copy(ysend.at[c, k, at], recv[c].at[k, at], ys.at[i, k], yr.at[i, k], along(CENTRE - k)))
            group[-1].start()
        answers.append(group)

    for one in loads[3:] + table_loads:
        one.wait()
    half = len(CUTS)
    prepare(0, route, kc, pick, pick2, deg, rev, term, prow, alpha, square, toep)
    for one in asks:
        one.wait_recv()
    for i in range(half):
        answer(i)
    prepare(1, route, kc, pick, pick2, deg, rev, term, prow, alpha, square, toep)
    for i in range(half, 2 * half):
        answer(i)
    for c in range(2):
        recv[c][CENTRE] = chosen(CENTRE, c, 0, PACKED)

    for group in answers[:half]:
        for one in group:
            one.wait_recv()
    fill_lhs([recv_flux[route[t, 0]] for t in range(2)], lhs)
    hbuf[...] = jnp.dot(lhs[...], ca[...], preferred_element_type=F32)
    mix_columns(route, hbuf, alpha, uh, ul)
    z = jnp.dot(rh[...], uh[...], preferred_element_type=F32)
    z = z[0:128] + z[128:256] + jnp.dot(rh[0:128, :], ul[...], preferred_element_type=F32)
    stores = []

    def keep(c, t, value):
        result[c, t] = value
        stores.append(pltpu.make_async_copy(result.at[c, t], out.at[t, c], out_sem.at[c, t]))
        stores[-1].start()

    for t in range(2):
        keep(0, t, sci[0, t] - z[:, t * TILE : (t + 1) * TILE])
    for group in answers[half:]:
        for one in group:
            one.wait_recv()
    fill_lhs([recv_var[route[t, 0]] for t in range(2)], lhs)
    for t in range(2):
        keep(1, t, sci[1, t] + variance(t, lhs, toep))
    for one in stores:
        one.wait()
    for one in asks + sum(gathers, []) + sum(answers, []):
        one.wait_send()


def per_device(science_flux, science_var, templ_flux, templ_var, kernel_coefs, tile_route):
    hbm = pl.BlockSpec(memory_space=pl.ANY)
    dma = pltpu.SemaphoreType.DMA
    tables = [jnp.asarray(x) for x in make_tables()]
    n = 2 * len(CUTS)
    out = pl.pallas_call(
        difference_kernel,
        out_shape=jax.ShapeDtypeStruct((2, 2, TILE, TILE), F32),
        in_specs=[hbm] * (6 + N_TABLES),
        out_specs=hbm,
        scratch_shapes=[
            pltpu.VMEM((2, PAD, PAD), F32),
            pltpu.SMEM((2, 5), jnp.int32),
            pltpu.VMEM((kernel_coefs.shape[1], 1, COLS), F32),
            pltpu.VMEM((2, 2, TILE, TILE), F32),
            pltpu.VMEM((2, 2, TILE, TILE), F32),
        ]
        + [pltpu.VMEM(x.shape, x.dtype) for x in tables]
        + [
            pltpu.VMEM((2, 4, PACKED, TILE), F32),
            pltpu.VMEM((2, 5, PACKED, TILE), F32),
            pltpu.VMEM((5, PACKED, TILE), F32),
            pltpu.VMEM((5, PACKED, TILE), F32),
            pltpu.VMEM((5, 8, TILE), jnp.int32),
            pltpu.VMEM((5, 8, TILE), jnp.int32),
            pltpu.VMEM((2 * ROWS, 512), BF16),
            pltpu.VMEM((2, 96, TILE), F32),
            pltpu.VMEM((2, 24, TILE), F32),
            pltpu.VMEM((2, 512, 24 * TILE), BF16),
            pltpu.VMEM((2 * ROWS, 1024), F32),
            pltpu.VMEM((2 * DEGREES * ROWS, 256), BF16),
            pltpu.VMEM((2 * DEGREES * ROWS, 256), BF16),
            dma((6,)),
            dma((N_TABLES,)),
            dma((2, 2)),
            dma((n, 4)),
            dma((n, 4)),
            dma((n, 5)),
            dma((n, 5)),
            dma((5,)),
            dma((5,)),
        ],
        compiler_params=pltpu.CompilerParams(
            collective_id=0, has_side_effects=True, vmem_limit_bytes=63 * 2**20
        ),
        name="difference",
    )(
        templ_flux[0].transpose(1, 0, 2),
        templ_var[0].transpose(1, 0, 2),
        tile_route[0],
        kernel_coefs.transpose(1, 0, 2),
        science_flux[0],
        science_var[0],
        *tables,
    )
    return out[None]


def solution(mesh):
    return jax.shard_map(
        per_device,
        mesh=mesh,
        in_specs=(
            P("exp", "patch", None, None),
            P("exp", "patch", None, None),
            P("patch", "exp", None, None),
            P("patch", "exp", None, None),
            P("exp", None, None),
            P("exp", "patch", None),
        ),
        out_specs=P("exp", "patch", None, None, None),
        check_vma=False,
    )
```

```python
import jax
import jax.numpy as jnp
import ml_dtypes
import numpy as np
from jax import lax
from jax.experimental import pallas as pl
from jax.experimental.pallas import tpu as pltpu
from jax.sharding import PartitionSpec as P

TILE = 128
HALF = 11
KSIZE = 23
PAD = 150
BASES = 32
TERMS = 6
DET_SIDE = 32
COLS = BASES * TERMS
MAIN = 152
REM = PAD - TILE
PACKED = MAIN + 32
GROUPS = 5
ROWS = 160
CUTS = ((0, 96), (96, PACKED))
N_TABLES = 8
CENTRE = 2
SCALE = TILE * DET_SIDE * 0.5
DEGREES = 6
MESH = pl.DeviceIdType.MESH
BF16 = jnp.bfloat16
F32 = jnp.float32
HIGH = lax.Precision.HIGHEST


def split_np(x):
    hi = x.astype(np.float32).astype(ml_dtypes.bfloat16)
    lo = (x - hi.astype(np.float64)).astype(ml_dtypes.bfloat16)
    return hi, lo


def power_profile(s, m):
    ratio = (np.arange(KSIZE) - HALF) / (1.5 + 1.5 * s)
    return ratio**m * np.exp(-0.5 * ratio * ratio)


def step_up(s, m):
    return (1.5 + 1.5 * s) * np.abs(power_profile(s, m + 1)).sum() / np.abs(power_profile(s, m)).sum()


def banded(profiles):
    out = np.zeros((len(profiles), PAD, TILE))
    for u in range(KSIZE):
        for x in range(TILE):
            out[:, x + u, x] = profiles[:, u]
    return out


def make_tables():
    prof = np.zeros((8, KSIZE))
    wide = np.zeros((2 * DEGREES, KSIZE))
    for s in range(2):
        for m in range(DEGREES):
            row = power_profile(s, m)
            wide[s * DEGREES + m] = row / np.abs(row).sum()
        prof[s * 4 : s * 4 + 4] = wide[s * DEGREES : s * DEGREES + 4]
    toep = banded(prof)
    cols = toep.transpose(1, 0, 2).reshape(PAD, 8 * TILE)
    hi, lo = split_np(cols)
    ca = np.zeros((4 * TILE, 8 * TILE), ml_dtypes.bfloat16)
    ca[0:128] = hi[:128]
    ca[128:256] = hi[:128]
    ca[256:384] = lo[:128]
    ca[384 : 384 + REM] = hi[128:]
    ca[416 : 416 + REM] = hi[128:]
    ca[448 : 448 + REM] = lo[128:]
    rows = np.zeros((TILE, 2 * DEGREES, ROWS))
    rows[:, :, :PAD] = banded(wide).transpose(2, 0, 1)
    hi, lo = split_np(rows.reshape(TILE, 2 * DEGREES * ROWS))
    rh = np.concatenate([hi, lo], 0)
    xdeg = [0, 1, 0, 2, 1, 0]
    ydeg = [0, 0, 1, 0, 1, 2]
    pick = np.zeros((96, COLS), np.float32)
    pick2 = np.zeros((8, COLS), np.float32)
    deg = np.zeros((COLS, TILE), np.float32)
    rev = np.zeros((COLS, TILE), np.float32)
    term = np.zeros((8, COLS), np.float32)
    for b in range(BASES):
        s, mx, my = b % 2, b // 2 % 4, b // 8 % 4
        for k in range(TERMS):
            col = b * TERMS + k
            pick[((s * 4 + mx) * 3 + ydeg[k]) * 4 + my, col] = 1
            pick2[s * 4 + mx, col] = 1
            deg[col] = xdeg[k]
            term[:, col] = k
            for v in range(KSIZE):
                rev[col, -v % TILE] = prof[s * 4 + my, v]
    prow = np.zeros((24, 8), np.float32)
    prow[:KSIZE] = prof.T
    return ca, rh, pick, pick2, deg, rev, term, prow


def fill_lhs(tiles, dst):
    lane = lax.broadcasted_iota(jnp.int32, (32, TILE), 1)
    pieces = []
    for src in tiles:
        main = jnp.concatenate([src[0:MAIN], jnp.zeros((ROWS - MAIN, TILE), F32)], 0)
        hi = main.astype(BF16)
        lo = (main - hi.astype(F32)).astype(BF16)
        other = src[MAIN:PACKED]
        parts = []
        for g in range(GROUPS):
            part = pltpu.roll(other, TILE - REM * g, 1) if g else other
            part = jnp.where(lane < REM, part, 0.0)
            top = part.astype(BF16).astype(F32)
            parts.append((top + pltpu.roll(part - top, 32, 1) + pltpu.roll(top, 64, 1)).astype(BF16))
        pieces.append((hi, lo, jnp.concatenate(parts, 0)))
    for t, (hi, lo, rest) in enumerate(pieces):
        at = slice(t * ROWS, (t + 1) * ROWS)
        dst[at, 0:128] = hi
        dst[at, 128:256] = lo
        dst[at, 256:384] = hi
        dst[at, 384:512] = rest


def prepare(t, route, kc, pick, pick2, deg, rev, term, prow, alpha, square, toep):
    coefs = kc[route[t, 4]]
    row = route[t, 2].astype(F32)
    col = route[t, 3].astype(F32)
    lanes = lax.broadcasted_iota(jnp.int32, (1, TILE), 1).astype(F32)
    xs = (col * TILE + lanes + 0.5) / SCALE - 1.0
    powers = jnp.where(deg[...] == 0.0, 1.0, jnp.where(deg[...] == 1.0, xs, xs * xs))
    rows = jnp.dot(pick[...] * coefs, powers, precision=HIGH, preferred_element_type=F32)
    alpha[t] = jnp.broadcast_to(rows[:, None, :], (96, 8, TILE))
    cx = (col * TILE + TILE * 0.5) / SCALE - 1.0
    cy = (row * TILE + TILE * 0.5) / SCALE - 1.0
    kinds = term[...]
    centre = jnp.where(kinds == 0.0, 1.0, 0.0)
    for k, value in enumerate((cx, cy, cx * cx, cx * cy, cy * cy)):
        centre = jnp.where(kinds == k + 1.0, value, centre)
    mixed = jnp.dot(pick2[...] * centre * coefs, rev[...], precision=HIGH, preferred_element_type=F32)
    kernel = jnp.dot(prow[...], mixed, precision=HIGH, preferred_element_type=F32)
    sub = lax.broadcasted_iota(jnp.int32, (32, TILE), 0)
    lane = lax.broadcasted_iota(jnp.int32, (32, TILE), 1)
    low = lane <= sub
    square[t] = kernel * kernel

    def lag(u, carry):
        at = pl.ds(pl.multiple_of((lax.rem(u, 8) * 3 + lax.div(u, 8)) * TILE, TILE), TILE)
        base = jnp.broadcast_to(square[t, pl.ds(u, 1), :], (TILE, TILE))
        circ = pltpu.roll(base, 0, 1, stride=1, stride_axis=0)
        top = circ[0:32]
        main = jnp.concatenate([jnp.where(low, top, 0.0), circ[32:]], 0)
        rest = jnp.where(low, 0.0, top)
        hi = main.astype(BF16)
        toep[t, 0:128, at] = hi
        toep[t, 128:256, at] = hi
        toep[t, 256:384, at] = (main - hi.astype(F32)).astype(BF16)
        hi = rest.astype(BF16)
        toep[t, 384:416, at] = hi
        toep[t, 416:448, at] = hi
        toep[t, 448:480, at] = (rest - hi.astype(F32)).astype(BF16)
        toep[t, 480:512, at] = jnp.zeros((32, TILE), BF16)
        return carry

    lax.fori_loop(0, KSIZE, lag, 0)


def fill_maps(t, route, alpha, maps):
    subs = lax.broadcasted_iota(jnp.int32, (8, TILE), 0).astype(F32)
    row = route[t, 2].astype(F32) * TILE + (0.5 - HALF)

    def chunk(i, carry):
        yc = (subs + (row + (i * 8).astype(F32))) / SCALE - 1.0
        twice = 2.0 * yc
        at = pl.ds(pl.multiple_of(i * 8, 8), 8)
        for s in range(2):
            for my in range(4):
                abc = [[alpha[t, ((s * 4 + mx) * 3 + j) * 4 + my] for j in range(3)] for mx in range(4)]
                for m in range(DEGREES):
                    total = None
                    if m < 4:
                        a, b, c = abc[m]
                        total = a + yc * (b + yc * c)
                    if 1 <= m <= 4:
                        a, b, c = abc[m - 1]
                        term = (b + twice * c) * np.float32(-step_up(s, m - 1) / SCALE)
                        total = term if total is None else total + term
                    if m >= 2:
                        a, b, c = abc[m - 2]
                        term = c * np.float32(step_up(s, m - 2) * step_up(s, m - 1) / SCALE**2)
                        total = term if total is None else total + term
                    maps[t, s * DEGREES + m, my, at, :] = total
        return carry

    lax.fori_loop(0, ROWS // 8, chunk, 0)


def mix_columns(hbuf, maps, uh, ul):
    def chunk(i, carry):
        at = pl.ds(pl.multiple_of(i * 16, 16), 16)
        for t in range(2):
            here = pl.ds(pl.multiple_of(t * ROWS + i * 16, 16), 16)
            for s in range(2):
                parts = [hbuf[here, (s * 4 + my) * TILE : (s * 4 + my + 1) * TILE] for my in range(4)]
                for m in range(DEGREES):
                    q = s * DEGREES + m
                    total = maps[t, q, 0, at, :] * parts[0]
                    for my in range(1, 4):
                        total = total + maps[t, q, my, at, :] * parts[my]
                    to = pl.ds(pl.multiple_of(q * ROWS + i * 16, 16), 16)
                    cols = slice(t * TILE, (t + 1) * TILE)
                    hi = total.astype(BF16)
                    uh[to, cols] = hi
                    ul[to, cols] = (total - hi.astype(F32)).astype(BF16)
        return carry

    lax.fori_loop(0, ROWS // 16, chunk, 0)


def variance(t, lhs, toep):
    acc = jnp.zeros((TILE, TILE), F32)
    for r in range(0, 8, 2):
        width = 768 if r < 6 else 640
        part = jnp.dot(
            lhs[t * ROWS : (t + 1) * ROWS, :], toep[t, :, r * 384 : r * 384 + width], preferred_element_type=F32
        )
        for k in range(2):
            at = k * 384
            total = part[0:136, at : at + 128] + part[8:144, at + 128 : at + 256]
            if at + 384 <= width:
                total = total + part[16:152, at + 256 : at + 384]
            acc = acc + total[r + k : r + k + TILE]
    return acc


def fetch(refs, buffers, sem):
    copies = [pltpu.make_async_copy(src, dst, sem.at[i]) for i, (src, dst) in enumerate(zip(refs, buffers))]
    for one in copies:
        one.start()
    return copies


def pack(raw, dst):
    dst[0:PAD, :] = raw[:, 0:TILE]
    dst[PAD:MAIN, :] = jnp.zeros((MAIN - PAD, TILE), F32)
    packed = jnp.zeros((32, TILE), F32)
    for g in range(GROUPS):
        n = min(32, PAD - 32 * g)
        part = raw[32 * g : 32 * g + n, TILE:PAD]
        part = jnp.concatenate([part, jnp.zeros((n, TILE - REM), F32)], 1)
        if n < 32:
            part = jnp.concatenate([part, jnp.zeros((32 - n, TILE), F32)], 0)
        if g:
            part = pltpu.roll(part, REM * g, 1)
        packed = packed + part
    dst[MAIN:PACKED, :] = packed


def difference_kernel(*refs):
    n = N_TABLES
    tf, tv, route_in, kc_in, sf_in, sv_in = refs[:6]
    tables_in, out = refs[6 : 6 + n], refs[6 + n]
    raw, route, kc, sci, result = refs[7 + n : 12 + n]
    tables = refs[12 + n : 12 + 2 * n]
    gath, ysend, recv_flux, recv_var, rqs, rqr, lhs, alpha, maps, square, toep, hbuf, uh, ul = refs[12 + 2 * n : 26 + 2 * n]
    ld_sem, tab_sem, out_sem, xs, xr, ys, yr, rs, rr = refs[26 + 2 * n :]
    recv = (recv_flux, recv_var)
    ca, rh, pick, pick2, deg, rev, term, prow = tables

    e = lax.axis_index("exp")
    p = lax.axis_index("patch")
    ne = lax.axis_size("exp")
    npatch = lax.axis_size("patch")
    exposures = {k: (lax.rem(e + k, ne), p) for k in (2, 1, 3)}

    def along(d):
        return (e, lax.rem(p + d + npatch, npatch))

    barrier = pltpu.get_barrier_semaphore()
    others = list(exposures.values()) + [along(d) for d in (-2, -1, 1, 2)]
    for other in others:
        pl.semaphore_signal(barrier, inc=1, device_id=other, device_id_type=MESH)
    loads = fetch(
        (tf.at[:, 0, :], tv.at[:, 0, :], route_in, kc_in, sf_in, sv_in),
        (raw.at[0], raw.at[1], route, kc, sci.at[0], sci.at[1]),
        ld_sem,
    )
    table_loads = fetch(tables_in, tables, tab_sem)
    loads[2].wait()
    for k in range(5):
        want = jnp.int32(0)
        for t in range(2):
            want = jnp.where(route[t, 0] == k, route[t, 1], want)
        rqs[k] = jnp.full((8, TILE), lax.rem(want - e + ne, ne), jnp.int32)
    for c in range(2):
        loads[c].wait()
        pack(raw.at[c], gath.at[c, 0])
    pl.semaphore_wait(barrier, len(others))

    def copy(src, dst, ssem, rsem, to):
        return pltpu.make_async_remote_copy(
            src_ref=src, dst_ref=dst, send_sem=ssem, recv_sem=rsem, device_id=to, device_id_type=MESH
        )

    chunks = [(c, lo, hi) for c in range(2) for lo, hi in CUTS]
    gathers, answers, asks = [], [], []
    for i, (c, lo, hi) in enumerate(chunks):
        at = pl.ds(lo, hi - lo)
        group = [
            copy(gath.at[c, 0, at], gath.at[c, 4 - k, at], xs.at[i, k], xr.at[i, k], to) for k, to in exposures.items()
        ]
        for one in group:
            one.start()
        gathers.append(group)
        if i == 0:
            for d in (-2, -1, 1, 2):
                k = d + CENTRE
                asks.append(copy(rqs.at[k], rqr.at[k], rs.at[k], rr.at[k], along(d)))
                asks[-1].start()

    def chosen(k, c, lo, hi):
        asked = rqr[k, 0:1, :] if k != CENTRE else rqs[k, 0:1, :]
        asked = jnp.broadcast_to(asked, (hi - lo, TILE))
        value = gath[c, 3, lo:hi]
        for j in (2, 1, 0):
            value = jnp.where(asked == j, gath[c, j, lo:hi], value)
        return value

    def answer(i):
        c, lo, hi = chunks[i]
        at = pl.ds(lo, hi - lo)
        for one in gathers[i]:
            one.wait_recv()
        group = []
        for k in (0, 4, 1, 3):
            ysend[c, k, lo:hi] = chosen(k, c, lo, hi)
            group.append(copy(ysend.at[c, k, at], recv[c].at[k, at], ys.at[i, k], yr.at[i, k], along(CENTRE - k)))
            group[-1].start()
        answers.append(group)

    for one in loads[3:] + table_loads:
        one.wait()
    half = len(CUTS)
    for t in range(2):
        prepare(t, route, kc, pick, pick2, deg, rev, term, prow, alpha, square, toep)
    for one in asks:
        one.wait_recv()
    for i in range(half):
        answer(i)
    last = p >= npatch - 2

    @pl.when(jnp.logical_not(last))
    def _():
        for t in range(2):
            fill_maps(t, route, alpha, maps)

    for i in range(half, 2 * half):
        answer(i)

    @pl.when(last)
    def _():
        for t in range(2):
            fill_maps(t, route, alpha, maps)

    for c in range(2):
        recv[c][CENTRE] = chosen(CENTRE, c, 0, PACKED)

    for group in answers[:half]:
        for one in group:
            one.wait_recv()
    fill_lhs([recv_flux[route[t, 0]] for t in range(2)], lhs)
    hbuf[...] = jnp.dot(lhs[...], ca[...], preferred_element_type=F32)
    mix_columns(hbuf, maps, uh, ul)
    z = jnp.dot(rh[...], uh[...], preferred_element_type=F32)
    z = z[0:128] + z[128:256] + jnp.dot(rh[0:128, :], ul[...], preferred_element_type=F32)
    stores = []

    def keep(c, t, value):
        result[c, t] = value
        stores.append(pltpu.make_async_copy(result.at[c, t], out.at[t, c], out_sem.at[c, t]))
        stores[-1].start()

    for t in range(2):
        keep(0, t, sci[0, t] - z[:, t * TILE : (t + 1) * TILE])
    for group in answers[half:]:
        for one in group:
            one.wait_recv()
    fill_lhs([recv_var[route[t, 0]] for t in range(2)], lhs)
    for t in range(2):
        keep(1, t, sci[1, t] + variance(t, lhs, toep))
    for one in stores:
        one.wait()
    for one in asks + sum(gathers, []) + sum(answers, []):
        one.wait_send()


def per_device(science_flux, science_var, templ_flux, templ_var, kernel_coefs, tile_route):
    hbm = pl.BlockSpec(memory_space=pl.ANY)
    dma = pltpu.SemaphoreType.DMA
    tables = [jnp.asarray(x) for x in make_tables()]
    n = 2 * len(CUTS)
    out = pl.pallas_call(
        difference_kernel,
        out_shape=jax.ShapeDtypeStruct((2, 2, TILE, TILE), F32),
        in_specs=[hbm] * (6 + N_TABLES),
        out_specs=hbm,
        scratch_shapes=[
            pltpu.VMEM((2, PAD, PAD), F32),
            pltpu.SMEM((2, 5), jnp.int32),
            pltpu.VMEM((kernel_coefs.shape[1], 1, COLS), F32),
            pltpu.VMEM((2, 2, TILE, TILE), F32),
            pltpu.VMEM((2, 2, TILE, TILE), F32),
        ]
        + [pltpu.VMEM(x.shape, x.dtype) for x in tables]
        + [
            pltpu.VMEM((2, 4, PACKED, TILE), F32),
            pltpu.VMEM((2, 5, PACKED, TILE), F32),
            pltpu.VMEM((5, PACKED, TILE), F32),
            pltpu.VMEM((5, PACKED, TILE), F32),
            pltpu.VMEM((5, 8, TILE), jnp.int32),
            pltpu.VMEM((5, 8, TILE), jnp.int32),
            pltpu.VMEM((2 * ROWS, 512), BF16),
            pltpu.VMEM((2, 96, 8, TILE), F32),
            pltpu.VMEM((2, 2 * DEGREES, 4, ROWS, TILE), F32),
            pltpu.VMEM((2, 24, TILE), F32),
            pltpu.VMEM((2, 512, 24 * TILE), BF16),
            pltpu.VMEM((2 * ROWS, 1024), F32),
            pltpu.VMEM((2 * DEGREES * ROWS, 256), BF16),
            pltpu.VMEM((2 * DEGREES * ROWS, 256), BF16),
            dma((6,)),
            dma((N_TABLES,)),
            dma((2, 2)),
            dma((n, 4)),
            dma((n, 4)),
            dma((n, 5)),
            dma((n, 5)),
            dma((5,)),
            dma((5,)),
        ],
        compiler_params=pltpu.CompilerParams(
            collective_id=0, has_side_effects=True, vmem_limit_bytes=63 * 2**20
        ),
        name="difference",
    )(
        templ_flux[0].transpose(1, 0, 2),
        templ_var[0].transpose(1, 0, 2),
        tile_route[0],
        kernel_coefs.transpose(1, 0, 2),
        science_flux[0],
        science_var[0],
        *tables,
    )
    return out[None]


def solution(mesh):
    return jax.shard_map(
        per_device,
        mesh=mesh,
        in_specs=(
            P("exp", "patch", None, None),
            P("exp", "patch", None, None),
            P("patch", "exp", None, None),
            P("patch", "exp", None, None),
            P("exp", None, None),
            P("exp", "patch", None),
        ),
        out_specs=P("exp", "patch", None, None, None),
        check_vma=False,
    )
```

```python
import jax
import jax.numpy as jnp
import ml_dtypes
import numpy as np
from jax import lax
from jax.experimental import pallas as pl
from jax.experimental.pallas import tpu as pltpu
from jax.sharding import PartitionSpec as P

TILE = 128
HALF = 11
KSIZE = 23
PAD = 150
BASES = 32
TERMS = 6
DET_SIDE = 32
COLS = BASES * TERMS
MAIN = 152
REM = PAD - TILE
PACKED = MAIN + 32
GROUPS = 5
ROWS = 160
CUTS = ((0, 96), (96, PACKED))
N_TABLES = 8
CENTRE = 2
SCALE = TILE * DET_SIDE * 0.5
DEGREES = 6
MESH = pl.DeviceIdType.MESH
BF16 = jnp.bfloat16
F32 = jnp.float32
HIGH = lax.Precision.HIGHEST


def split_np(x):
    hi = x.astype(np.float32).astype(ml_dtypes.bfloat16)
    lo = (x - hi.astype(np.float64)).astype(ml_dtypes.bfloat16)
    return hi, lo


def power_profile(s, m):
    ratio = (np.arange(KSIZE) - HALF) / (1.5 + 1.5 * s)
    return ratio**m * np.exp(-0.5 * ratio * ratio)


def step_up(s, m):
    return (1.5 + 1.5 * s) * np.abs(power_profile(s, m + 1)).sum() / np.abs(power_profile(s, m)).sum()


def banded(profiles):
    out = np.zeros((len(profiles), PAD, TILE))
    for u in range(KSIZE):
        for x in range(TILE):
            out[:, x + u, x] = profiles[:, u]
    return out


def make_tables():
    prof = np.zeros((8, KSIZE))
    wide = np.zeros((2 * DEGREES, KSIZE))
    for s in range(2):
        for m in range(DEGREES):
            row = power_profile(s, m)
            wide[s * DEGREES + m] = row / np.abs(row).sum()
        prof[s * 4 : s * 4 + 4] = wide[s * DEGREES : s * DEGREES + 4]
    toep = banded(prof)
    cols = toep.transpose(1, 0, 2).reshape(PAD, 8 * TILE)
    hi, lo = split_np(cols)
    ca = np.zeros((4 * TILE, 8 * TILE), ml_dtypes.bfloat16)
    ca[0:128] = hi[:128]
    ca[128:256] = hi[:128]
    ca[256:384] = lo[:128]
    ca[384 : 384 + REM] = hi[128:]
    ca[416 : 416 + REM] = hi[128:]
    ca[448 : 448 + REM] = lo[128:]
    rows = np.zeros((TILE, 2 * DEGREES, ROWS))
    rows[:, :, :PAD] = banded(wide).transpose(2, 0, 1)
    hi, lo = split_np(rows.reshape(TILE, 2 * DEGREES * ROWS))
    rh = np.concatenate([hi, lo], 0)
    xdeg = [0, 1, 0, 2, 1, 0]
    ydeg = [0, 0, 1, 0, 1, 2]
    pick = np.zeros((96, COLS), np.float32)
    pick2 = np.zeros((8, COLS), np.float32)
    deg = np.zeros((COLS, TILE), np.float32)
    rev = np.zeros((COLS, TILE), np.float32)
    term = np.zeros((8, COLS), np.float32)
    for b in range(BASES):
        s, mx, my = b % 2, b // 2 % 4, b // 8 % 4
        for k in range(TERMS):
            col = b * TERMS + k
            pick[((s * 4 + mx) * 3 + ydeg[k]) * 4 + my, col] = 1
            pick2[s * 4 + mx, col] = 1
            deg[col] = xdeg[k]
            term[:, col] = k
            for v in range(KSIZE):
                rev[col, -v % TILE] = prof[s * 4 + my, v]
    prow = np.zeros((24, 8), np.float32)
    prow[:KSIZE] = prof.T
    return ca, rh, pick, pick2, deg, rev, term, prow


def fill_lhs(tiles, dst):
    lane = lax.broadcasted_iota(jnp.int32, (32, TILE), 1)
    pieces = []
    for src in tiles:
        main = jnp.concatenate([src[0:MAIN], jnp.zeros((ROWS - MAIN, TILE), F32)], 0)
        hi = main.astype(BF16)
        lo = (main - hi.astype(F32)).astype(BF16)
        other = src[MAIN:PACKED]
        parts = []
        for g in range(GROUPS):
            part = pltpu.roll(other, TILE - REM * g, 1) if g else other
            part = jnp.where(lane < REM, part, 0.0)
            top = part.astype(BF16).astype(F32)
            parts.append((top + pltpu.roll(part - top, 32, 1) + pltpu.roll(top, 64, 1)).astype(BF16))
        pieces.append((hi, lo, jnp.concatenate(parts, 0)))
    for t, (hi, lo, rest) in enumerate(pieces):
        at = slice(t * ROWS, (t + 1) * ROWS)
        dst[at, 0:128] = hi
        dst[at, 128:256] = lo
        dst[at, 256:384] = hi
        dst[at, 384:512] = rest


def prepare(t, route, kc, pick, pick2, deg, rev, term, prow, alpha, square, toep):
    coefs = kc[route[t, 4]]
    row = route[t, 2].astype(F32)
    col = route[t, 3].astype(F32)
    lanes = lax.broadcasted_iota(jnp.int32, (1, TILE), 1).astype(F32)
    xs = (col * TILE + lanes + 0.5) / SCALE - 1.0
    powers = jnp.where(deg[...] == 0.0, 1.0, jnp.where(deg[...] == 1.0, xs, xs * xs))
    rows = jnp.dot(pick[...] * coefs, powers, precision=HIGH, preferred_element_type=F32)
    alpha[t] = jnp.broadcast_to(rows[:, None, :], (96, 8, TILE))
    cx = (col * TILE + TILE * 0.5) / SCALE - 1.0
    cy = (row * TILE + TILE * 0.5) / SCALE - 1.0
    kinds = term[...]
    centre = jnp.where(kinds == 0.0, 1.0, 0.0)
    for k, value in enumerate((cx, cy, cx * cx, cx * cy, cy * cy)):
        centre = jnp.where(kinds == k + 1.0, value, centre)
    mixed = jnp.dot(pick2[...] * centre * coefs, rev[...], precision=HIGH, preferred_element_type=F32)
    kernel = jnp.dot(prow[...], mixed, precision=HIGH, preferred_element_type=F32)
    sub = lax.broadcasted_iota(jnp.int32, (32, TILE), 0)
    lane = lax.broadcasted_iota(jnp.int32, (32, TILE), 1)
    low = lane <= sub
    square[t] = kernel * kernel

    def lag(u, carry):
        at = pl.ds(pl.multiple_of((lax.rem(u, 8) * 3 + lax.div(u, 8)) * TILE, TILE), TILE)
        base = jnp.broadcast_to(square[t, pl.ds(u, 1), :], (TILE, TILE))
        circ = pltpu.roll(base, 0, 1, stride=1, stride_axis=0)
        top = circ[0:32]
        main = jnp.concatenate([jnp.where(low, top, 0.0), circ[32:]], 0)
        rest = jnp.where(low, 0.0, top)
        hi = main.astype(BF16)
        toep[t, 0:128, at] = hi
        toep[t, 128:256, at] = hi
        toep[t, 256:384, at] = (main - hi.astype(F32)).astype(BF16)
        hi = rest.astype(BF16)
        toep[t, 384:416, at] = hi
        toep[t, 416:448, at] = hi
        toep[t, 448:480, at] = (rest - hi.astype(F32)).astype(BF16)
        toep[t, 480:512, at] = jnp.zeros((32, TILE), BF16)
        return carry

    lax.fori_loop(0, KSIZE, lag, 0)


def fill_maps(t, route, alpha, maps):
    subs = lax.broadcasted_iota(jnp.int32, (8, TILE), 0).astype(F32)
    row = route[t, 2].astype(F32) * TILE + (0.5 - HALF)

    def chunk(i, carry):
        yc = (subs + (row + (i * 8).astype(F32))) / SCALE - 1.0
        twice = 2.0 * yc
        at = pl.ds(pl.multiple_of(i * 8, 8), 8)
        for s in range(2):
            for my in range(4):
                abc = [[alpha[t, ((s * 4 + mx) * 3 + j) * 4 + my] for j in range(3)] for mx in range(4)]
                for m in range(DEGREES):
                    total = None
                    if m < 4:
                        a, b, c = abc[m]
                        total = a + yc * (b + yc * c)
                    if 1 <= m <= 4:
                        a, b, c = abc[m - 1]
                        term = (b + twice * c) * np.float32(-step_up(s, m - 1) / SCALE)
                        total = term if total is None else total + term
                    if m >= 2:
                        a, b, c = abc[m - 2]
                        term = c * np.float32(step_up(s, m - 2) * step_up(s, m - 1) / SCALE**2)
                        total = term if total is None else total + term
                    maps[t, s * DEGREES + m, my, at, :] = total
        return carry

    lax.fori_loop(0, ROWS // 8, chunk, 0)


def mix_columns(hbuf, maps, uh, ul):
    def chunk(i, carry):
        at = pl.ds(pl.multiple_of(i * 16, 16), 16)
        for t in range(2):
            here = pl.ds(pl.multiple_of(t * ROWS + i * 16, 16), 16)
            for s in range(2):
                parts = [hbuf[here, (s * 4 + my) * TILE : (s * 4 + my + 1) * TILE] for my in range(4)]
                for m in range(DEGREES):
                    q = s * DEGREES + m
                    total = maps[t, q, 0, at, :] * parts[0]
                    for my in range(1, 4):
                        total = total + maps[t, q, my, at, :] * parts[my]
                    to = pl.ds(pl.multiple_of(q * ROWS + i * 16, 16), 16)
                    cols = slice(t * TILE, (t + 1) * TILE)
                    hi = total.astype(BF16)
                    uh[to, cols] = hi
                    ul[to, cols] = (total - hi.astype(F32)).astype(BF16)
        return carry

    lax.fori_loop(0, ROWS // 16, chunk, 0)


def variance(t, lhs, toep):
    acc = jnp.zeros((TILE, TILE), F32)
    for r in range(0, 8, 2):
        width = 768 if r < 6 else 640
        part = jnp.dot(
            lhs[t * ROWS : (t + 1) * ROWS, :], toep[t, :, r * 384 : r * 384 + width], preferred_element_type=F32
        )
        for k in range(2):
            at = k * 384
            total = part[0:136, at : at + 128] + part[8:144, at + 128 : at + 256]
            if at + 384 <= width:
                total = total + part[16:152, at + 256 : at + 384]
            acc = acc + total[r + k : r + k + TILE]
    return acc


def fetch(refs, buffers, sem):
    copies = [pltpu.make_async_copy(src, dst, sem.at[i]) for i, (src, dst) in enumerate(zip(refs, buffers))]
    for one in copies:
        one.start()
    return copies


def pack(raw, dst):
    dst[0:PAD, :] = raw[:, 0:TILE]
    dst[PAD:MAIN, :] = jnp.zeros((MAIN - PAD, TILE), F32)
    packed = jnp.zeros((32, TILE), F32)
    for g in range(GROUPS):
        n = min(32, PAD - 32 * g)
        part = raw[32 * g : 32 * g + n, TILE:PAD]
        part = jnp.concatenate([part, jnp.zeros((n, TILE - REM), F32)], 1)
        if n < 32:
            part = jnp.concatenate([part, jnp.zeros((32 - n, TILE), F32)], 0)
        if g:
            part = pltpu.roll(part, REM * g, 1)
        packed = packed + part
    dst[MAIN:PACKED, :] = packed


def difference_kernel(*refs):
    n = N_TABLES
    tf, tv, route_in, kc_in, sf_in, sv_in = refs[:6]
    tables_in, out = refs[6 : 6 + n], refs[6 + n]
    raw, route, kc, sci, result = refs[7 + n : 12 + n]
    tables = refs[12 + n : 12 + 2 * n]
    gath, ysend, recv_flux, recv_var, rqs, rqr, lhs, alpha, maps, square, toep, hbuf, uh, ul = refs[12 + 2 * n : 26 + 2 * n]
    ld_sem, tab_sem, out_sem, xs, xr, ys, yr, rs, rr = refs[26 + 2 * n :]
    recv = (recv_flux, recv_var)
    ca, rh, pick, pick2, deg, rev, term, prow = tables

    e = lax.axis_index("exp")
    p = lax.axis_index("patch")
    ne = lax.axis_size("exp")
    npatch = lax.axis_size("patch")
    exposures = {k: (lax.rem(e + k, ne), p) for k in (2, 1, 3)}

    def along(d):
        return (e, lax.rem(p + d + npatch, npatch))

    barrier = pltpu.get_barrier_semaphore()
    others = list(exposures.values()) + [along(d) for d in (-2, -1, 1, 2)]
    for other in others:
        pl.semaphore_signal(barrier, inc=1, device_id=other, device_id_type=MESH)
    loads = fetch(
        (tf.at[:, 0, :], tv.at[:, 0, :], route_in, kc_in, sf_in, sv_in),
        (raw.at[0], raw.at[1], route, kc, sci.at[0], sci.at[1]),
        ld_sem,
    )
    table_loads = fetch(tables_in, tables, tab_sem)
    loads[2].wait()
    for k in range(5):
        want = jnp.int32(0)
        for t in range(2):
            want = jnp.where(route[t, 0] == k, route[t, 1], want)
        rqs[k] = jnp.full((8, TILE), lax.rem(want - e + ne, ne), jnp.int32)
    for c in range(2):
        loads[c].wait()
        pack(raw.at[c], gath.at[c, 0])
    pl.semaphore_wait(barrier, len(others))

    def copy(src, dst, ssem, rsem, to):
        return pltpu.make_async_remote_copy(
            src_ref=src, dst_ref=dst, send_sem=ssem, recv_sem=rsem, device_id=to, device_id_type=MESH
        )

    chunks = [(c, lo, hi) for c in range(2) for lo, hi in CUTS]
    gathers, answers, asks = [], [], []
    for i, (c, lo, hi) in enumerate(chunks):
        at = pl.ds(lo, hi - lo)
        group = [
            copy(gath.at[c, 0, at], gath.at[c, 4 - k, at], xs.at[i, k], xr.at[i, k], to) for k, to in exposures.items()
        ]
        for one in group:
            one.start()
        gathers.append(group)
        if i == 0:
            for d in (-2, -1, 1, 2):
                k = d + CENTRE
                asks.append(copy(rqs.at[k], rqr.at[k], rs.at[k], rr.at[k], along(d)))
                asks[-1].start()

    def chosen(k, c, lo, hi):
        asked = rqr[k, 0:1, :] if k != CENTRE else rqs[k, 0:1, :]
        asked = jnp.broadcast_to(asked, (hi - lo, TILE))
        value = gath[c, 3, lo:hi]
        for j in (2, 1, 0):
            value = jnp.where(asked == j, gath[c, j, lo:hi], value)
        return value

    def answer(i):
        c, lo, hi = chunks[i]
        at = pl.ds(lo, hi - lo)
        for one in gathers[i]:
            one.wait_recv()
        group = []
        for k in (0, 4, 1, 3):
            ysend[c, k, lo:hi] = chosen(k, c, lo, hi)
            group.append(copy(ysend.at[c, k, at], recv[c].at[k, at], ys.at[i, k], yr.at[i, k], along(CENTRE - k)))
            group[-1].start()
        answers.append(group)

    for one in loads[3:] + table_loads:
        one.wait()
    half = len(CUTS)
    last = p >= npatch - 2

    def ready(t, carry):
        prepare(t, route, kc, pick, pick2, deg, rev, term, prow, alpha, square, toep)
        return carry

    @pl.when(jnp.logical_not(last))
    def _():
        lax.fori_loop(0, 2, ready, 0)

    for one in asks:
        one.wait_recv()
    for i in range(half):
        answer(i)

    @pl.when(jnp.logical_not(last))
    def _():
        for t in range(2):
            fill_maps(t, route, alpha, maps)

    for i in range(half, 2 * half):
        answer(i)

    @pl.when(last)
    def _():
        lax.fori_loop(0, 2, ready, 0)
        for t in range(2):
            fill_maps(t, route, alpha, maps)

    for c in range(2):
        recv[c][CENTRE] = chosen(CENTRE, c, 0, PACKED)

    for group in answers[:half]:
        for one in group:
            one.wait_recv()
    fill_lhs([recv_flux[route[t, 0]] for t in range(2)], lhs)
    hbuf[...] = jnp.dot(lhs[...], ca[...], preferred_element_type=F32)
    mix_columns(hbuf, maps, uh, ul)
    z = jnp.dot(rh[...], uh[...], preferred_element_type=F32)
    z = z[0:128] + z[128:256] + jnp.dot(rh[0:128, :], ul[...], preferred_element_type=F32)
    stores = []

    def keep(c, t, value):
        result[c, t] = value
        stores.append(pltpu.make_async_copy(result.at[c, t], out.at[t, c], out_sem.at[c, t]))
        stores[-1].start()

    for t in range(2):
        keep(0, t, sci[0, t] - z[:, t * TILE : (t + 1) * TILE])
    for group in answers[half:]:
        for one in group:
            one.wait_recv()
    fill_lhs([recv_var[route[t, 0]] for t in range(2)], lhs)
    for t in range(2):
        keep(1, t, sci[1, t] + variance(t, lhs, toep))
    for one in stores:
        one.wait()
    for one in asks + sum(gathers, []) + sum(answers, []):
        one.wait_send()


def per_device(science_flux, science_var, templ_flux, templ_var, kernel_coefs, tile_route):
    hbm = pl.BlockSpec(memory_space=pl.ANY)
    dma = pltpu.SemaphoreType.DMA
    tables = [jnp.asarray(x) for x in make_tables()]
    n = 2 * len(CUTS)
    out = pl.pallas_call(
        difference_kernel,
        out_shape=jax.ShapeDtypeStruct((2, 2, TILE, TILE), F32),
        in_specs=[hbm] * (6 + N_TABLES),
        out_specs=hbm,
        scratch_shapes=[
            pltpu.VMEM((2, PAD, PAD), F32),
            pltpu.SMEM((2, 5), jnp.int32),
            pltpu.VMEM((kernel_coefs.shape[1], 1, COLS), F32),
            pltpu.VMEM((2, 2, TILE, TILE), F32),
            pltpu.VMEM((2, 2, TILE, TILE), F32),
        ]
        + [pltpu.VMEM(x.shape, x.dtype) for x in tables]
        + [
            pltpu.VMEM((2, 4, PACKED, TILE), F32),
            pltpu.VMEM((2, 5, PACKED, TILE), F32),
            pltpu.VMEM((5, PACKED, TILE), F32),
            pltpu.VMEM((5, PACKED, TILE), F32),
            pltpu.VMEM((5, 8, TILE), jnp.int32),
            pltpu.VMEM((5, 8, TILE), jnp.int32),
            pltpu.VMEM((2 * ROWS, 512), BF16),
            pltpu.VMEM((2, 96, 8, TILE), F32),
            pltpu.VMEM((2, 2 * DEGREES, 4, ROWS, TILE), F32),
            pltpu.VMEM((2, 24, TILE), F32),
            pltpu.VMEM((2, 512, 24 * TILE), BF16),
            pltpu.VMEM((2 * ROWS, 1024), F32),
            pltpu.VMEM((2 * DEGREES * ROWS, 256), BF16),
            pltpu.VMEM((2 * DEGREES * ROWS, 256), BF16),
            dma((6,)),
            dma((N_TABLES,)),
            dma((2, 2)),
            dma((n, 4)),
            dma((n, 4)),
            dma((n, 5)),
            dma((n, 5)),
            dma((5,)),
            dma((5,)),
        ],
        compiler_params=pltpu.CompilerParams(
            collective_id=0, has_side_effects=True, vmem_limit_bytes=63 * 2**20
        ),
        name="difference",
    )(
        templ_flux[0].transpose(1, 0, 2),
        templ_var[0].transpose(1, 0, 2),
        tile_route[0],
        kernel_coefs.transpose(1, 0, 2),
        science_flux[0],
        science_var[0],
        *tables,
    )
    return out[None]


def solution(mesh):
    return jax.shard_map(
        per_device,
        mesh=mesh,
        in_specs=(
            P("exp", "patch", None, None),
            P("exp", "patch", None, None),
            P("patch", "exp", None, None),
            P("patch", "exp", None, None),
            P("exp", None, None),
            P("exp", "patch", None),
        ),
        out_specs=P("exp", "patch", None, None, None),
        check_vma=False,
    )
```

```python
import jax
import jax.numpy as jnp
import ml_dtypes
import numpy as np
from jax import lax
from jax.experimental import pallas as pl
from jax.experimental.pallas import tpu as pltpu
from jax.sharding import PartitionSpec as P

TILE = 128
HALF = 11
KSIZE = 23
PAD = 150
BASES = 32
TERMS = 6
DET_SIDE = 32
COLS = BASES * TERMS
MAIN = 152
REM = PAD - TILE
PACKED = MAIN + 32
GROUPS = 5
ROWS = 160
CUTS = ((0, 96), (96, PACKED))
N_TABLES = 3
VMEM_LIMIT = 54912 * 2**10
CENTRE = 2
SCALE = TILE * DET_SIDE * 0.5
DEGREES = 6
MESH = pl.DeviceIdType.MESH
BF16 = jnp.bfloat16
F32 = jnp.float32
HIGH = lax.Precision.HIGHEST


def split_np(x):
    hi = x.astype(np.float32).astype(ml_dtypes.bfloat16)
    lo = (x - hi.astype(np.float64)).astype(ml_dtypes.bfloat16)
    return hi, lo


def power_profile(s, m):
    ratio = (np.arange(KSIZE) - HALF) / (1.5 + 1.5 * s)
    return ratio**m * np.exp(-0.5 * ratio * ratio)


def step_up(s, m):
    return (1.5 + 1.5 * s) * np.abs(power_profile(s, m + 1)).sum() / np.abs(power_profile(s, m)).sum()


def banded(profiles):
    out = np.zeros((len(profiles), PAD, TILE))
    for u in range(KSIZE):
        for x in range(TILE):
            out[:, x + u, x] = profiles[:, u]
    return out


def make_tables():
    prof = np.zeros((8, KSIZE))
    wide = np.zeros((2 * DEGREES, KSIZE))
    for s in range(2):
        for m in range(DEGREES):
            row = power_profile(s, m)
            wide[s * DEGREES + m] = row / np.abs(row).sum()
        prof[s * 4 : s * 4 + 4] = wide[s * DEGREES : s * DEGREES + 4]
    toep = banded(prof)
    cols = toep.transpose(1, 0, 2).reshape(PAD, 8 * TILE)
    hi, lo = split_np(cols)
    ca = np.zeros((4 * TILE, 8 * TILE), ml_dtypes.bfloat16)
    ca[0:128] = hi[:128]
    ca[128:256] = hi[:128]
    ca[256:384] = lo[:128]
    ca[384 : 384 + REM] = hi[128:]
    ca[416 : 416 + REM] = hi[128:]
    ca[448 : 448 + REM] = lo[128:]
    rows = np.zeros((TILE, 2 * DEGREES, ROWS))
    rows[:, :, :PAD] = banded(wide).transpose(2, 0, 1)
    hi, lo = split_np(rows.reshape(TILE, 2 * DEGREES * ROWS))
    rh = np.concatenate([hi, lo], 0)
    xdeg = [0, 1, 0, 2, 1, 0]
    ydeg = [0, 0, 1, 0, 1, 2]
    pick = np.zeros((96, COLS), np.float32)
    pick2 = np.zeros((8, COLS), np.float32)
    deg = np.zeros((COLS, TILE), np.float32)
    rev = np.zeros((COLS, TILE), np.float32)
    term = np.zeros((8, COLS), np.float32)
    for b in range(BASES):
        s, mx, my = b % 2, b // 2 % 4, b // 8 % 4
        for k in range(TERMS):
            col = b * TERMS + k
            pick[((s * 4 + mx) * 3 + ydeg[k]) * 4 + my, col] = 1
            pick2[s * 4 + mx, col] = 1
            deg[col] = xdeg[k]
            term[:, col] = k
            for v in range(KSIZE):
                rev[col, -v % TILE] = prof[s * 4 + my, v]
    prow = np.zeros((24, 8), np.float32)
    prow[:KSIZE] = prof.T
    tab = np.zeros((328, 256), np.float32)
    tab[0:96, :COLS] = pick
    tab[96:104, :COLS] = pick2
    tab[104:112, :COLS] = term
    tab[112:304, 0:128] = deg
    tab[112:304, 128:256] = rev
    tab[304:328, 0:8] = prow
    return ca, rh, tab


def fill_lhs(tiles, dst):
    lane = lax.broadcasted_iota(jnp.int32, (32, TILE), 1)
    pieces = []
    for src in tiles:
        main = jnp.concatenate([src[0:MAIN], jnp.zeros((ROWS - MAIN, TILE), F32)], 0)
        hi = main.astype(BF16)
        lo = (main - hi.astype(F32)).astype(BF16)
        other = src[MAIN:PACKED]
        parts = []
        for g in range(GROUPS):
            part = pltpu.roll(other, TILE - REM * g, 1) if g else other
            part = jnp.where(lane < REM, part, 0.0)
            top = part.astype(BF16).astype(F32)
            parts.append((top + pltpu.roll(part - top, 32, 1) + pltpu.roll(top, 64, 1)).astype(BF16))
        pieces.append((hi, lo, jnp.concatenate(parts, 0)))
    for t, (hi, lo, rest) in enumerate(pieces):
        at = slice(t * ROWS, (t + 1) * ROWS)
        dst[at, 0:128] = hi
        dst[at, 128:256] = lo
        dst[at, 256:384] = hi
        dst[at, 384:512] = rest


def prepare(t, route, kc, pick, pick2, deg, rev, term, prow, alpha, square, toep):
    coefs = kc[route[t, 4]]
    row = route[t, 2].astype(F32)
    col = route[t, 3].astype(F32)
    lanes = lax.broadcasted_iota(jnp.int32, (1, TILE), 1).astype(F32)
    xs = (col * TILE + lanes + 0.5) / SCALE - 1.0
    powers = jnp.where(deg[...] == 0.0, 1.0, jnp.where(deg[...] == 1.0, xs, xs * xs))
    rows = jnp.dot(pick[...] * coefs, powers, precision=HIGH, preferred_element_type=F32)
    alpha[t] = jnp.broadcast_to(rows[:, None, :], (96, 8, TILE))
    cx = (col * TILE + TILE * 0.5) / SCALE - 1.0
    cy = (row * TILE + TILE * 0.5) / SCALE - 1.0
    kinds = term[...]
    centre = jnp.where(kinds == 0.0, 1.0, 0.0)
    for k, value in enumerate((cx, cy, cx * cx, cx * cy, cy * cy)):
        centre = jnp.where(kinds == k + 1.0, value, centre)
    mixed = jnp.dot(pick2[...] * centre * coefs, rev[...], precision=HIGH, preferred_element_type=F32)
    kernel = jnp.dot(prow[...], mixed, precision=HIGH, preferred_element_type=F32)
    sub = lax.broadcasted_iota(jnp.int32, (32, TILE), 0)
    lane = lax.broadcasted_iota(jnp.int32, (32, TILE), 1)
    low = lane <= sub
    square[t] = kernel * kernel

    def lag(u, carry):
        at = pl.ds(pl.multiple_of((lax.rem(u, 8) * 3 + lax.div(u, 8)) * TILE, TILE), TILE)
        base = jnp.broadcast_to(square[t, pl.ds(u, 1), :], (TILE, TILE))
        circ = pltpu.roll(base, 0, 1, stride=1, stride_axis=0)
        top = circ[0:32]
        main = jnp.concatenate([jnp.where(low, top, 0.0), circ[32:]], 0)
        rest = jnp.where(low, 0.0, top)
        hi = main.astype(BF16)
        toep[t, 0:128, at] = hi
        toep[t, 128:256, at] = hi
        toep[t, 256:384, at] = (main - hi.astype(F32)).astype(BF16)
        hi = rest.astype(BF16)
        toep[t, 384:416, at] = hi
        toep[t, 416:448, at] = hi
        toep[t, 448:480, at] = (rest - hi.astype(F32)).astype(BF16)
        toep[t, 480:512, at] = jnp.zeros((32, TILE), BF16)
        return carry

    lax.fori_loop(0, KSIZE, lag, 0)


def fill_maps(t, route, alpha, maps):
    subs = lax.broadcasted_iota(jnp.int32, (8, TILE), 0).astype(F32)
    row = route[t, 2].astype(F32) * TILE + (0.5 - HALF)

    def chunk(i, carry):
        yc = (subs + (row + (i * 8).astype(F32))) / SCALE - 1.0
        twice = 2.0 * yc
        at = pl.ds(pl.multiple_of(i * 8, 8), 8)
        for s in range(2):
            for my in range(4):
                abc = [[alpha[t, ((s * 4 + mx) * 3 + j) * 4 + my] for j in range(3)] for mx in range(4)]
                for m in range(DEGREES):
                    total = None
                    if m < 4:
                        a, b, c = abc[m]
                        total = a + yc * (b + yc * c)
                    if 1 <= m <= 4:
                        a, b, c = abc[m - 1]
                        term = (b + twice * c) * np.float32(-step_up(s, m - 1) / SCALE)
                        total = term if total is None else total + term
                    if m >= 2:
                        a, b, c = abc[m - 2]
                        term = c * np.float32(step_up(s, m - 2) * step_up(s, m - 1) / SCALE**2)
                        total = term if total is None else total + term
                    maps[t, s * DEGREES + m, my, at, :] = total
        return carry

    lax.fori_loop(0, ROWS // 8, chunk, 0)


def mix_columns(hbuf, maps, uh, ul):
    def chunk(i, carry):
        at = pl.ds(pl.multiple_of(i * 16, 16), 16)
        for t in range(2):
            here = pl.ds(pl.multiple_of(t * ROWS + i * 16, 16), 16)
            for s in range(2):
                parts = [hbuf[here, (s * 4 + my) * TILE : (s * 4 + my + 1) * TILE] for my in range(4)]
                for m in range(DEGREES):
                    q = s * DEGREES + m
                    total = maps[t, q, 0, at, :] * parts[0]
                    for my in range(1, 4):
                        total = total + maps[t, q, my, at, :] * parts[my]
                    to = pl.ds(pl.multiple_of(q * ROWS + i * 16, 16), 16)
                    cols = slice(t * TILE, (t + 1) * TILE)
                    hi = total.astype(BF16)
                    uh[to, cols] = hi
                    ul[to, cols] = (total - hi.astype(F32)).astype(BF16)
        return carry

    lax.fori_loop(0, ROWS // 16, chunk, 0)


def variance(t, lhs, toep):
    acc = jnp.zeros((TILE, TILE), F32)
    for r in range(0, 8, 2):
        width = 768 if r < 6 else 640
        part = jnp.dot(
            lhs[t * ROWS : (t + 1) * ROWS, :], toep[t, :, r * 384 : r * 384 + width], preferred_element_type=F32
        )
        for k in range(2):
            at = k * 384
            total = part[0:136, at : at + 128] + part[8:144, at + 128 : at + 256]
            if at + 384 <= width:
                total = total + part[16:152, at + 256 : at + 384]
            acc = acc + total[r + k : r + k + TILE]
    return acc


def fetch(refs, buffers, sem):
    copies = [pltpu.make_async_copy(src, dst, sem.at[i]) for i, (src, dst) in enumerate(zip(refs, buffers))]
    for one in copies:
        one.start()
    return copies


def pack(raw, dst):
    dst[0:PAD, :] = raw[:, 0:TILE]
    dst[PAD:MAIN, :] = jnp.zeros((MAIN - PAD, TILE), F32)
    packed = jnp.zeros((32, TILE), F32)
    for g in range(GROUPS):
        n = min(32, PAD - 32 * g)
        part = raw[32 * g : 32 * g + n, TILE:PAD]
        part = jnp.concatenate([part, jnp.zeros((n, TILE - REM), F32)], 1)
        if n < 32:
            part = jnp.concatenate([part, jnp.zeros((32 - n, TILE), F32)], 0)
        if g:
            part = pltpu.roll(part, REM * g, 1)
        packed = packed + part
    dst[MAIN:PACKED, :] = packed


def difference_kernel(*refs):
    n = N_TABLES
    tf, tv, route_in, kc_in, sf_in, sv_in = refs[:6]
    tables_in, outs = refs[6 : 6 + n], refs[6 + n : 10 + n]
    raw, route, kc, sci = refs[10 + n : 14 + n]
    tables = refs[14 + n : 14 + 2 * n]
    gath, ysend, recv_flux, recv_var, rqs, rqr, lhs, alpha, maps, square, toep, hbuf, uh, ul = refs[14 + 2 * n : 28 + 2 * n]
    ld_sem, tab_sem, xs, xr, ys, yr, rs, rr = refs[28 + 2 * n :]
    recv = (recv_flux, recv_var)
    ca, rh, tab = tables
    pick, pick2, term = (tab.at[lo:hi, 0:COLS] for lo, hi in ((0, 96), (96, 104), (104, 112)))
    deg, rev = tab.at[112:304, 0:128], tab.at[112:304, 128:256]
    prow = tab.at[304:328, 0:8]

    e = lax.axis_index("exp")
    p = lax.axis_index("patch")
    ne = lax.axis_size("exp")
    npatch = lax.axis_size("patch")
    exposures = {k: (lax.rem(e + k, ne), p) for k in (2, 1, 3)}

    def along(d):
        return (e, lax.rem(p + d + npatch, npatch))

    barrier = pltpu.get_barrier_semaphore()
    others = list(exposures.values()) + [along(d) for d in (-2, -1, 1, 2)]
    for other in others:
        pl.semaphore_signal(barrier, inc=1, device_id=other, device_id_type=MESH)
    loads = fetch(
        (tf.at[:, 0, :], tv.at[:, 0, :], route_in, kc_in, sf_in, sv_in),
        (raw.at[0], raw.at[1], route, kc, sci.at[0], sci.at[1]),
        ld_sem,
    )
    table_loads = fetch(tables_in, tables, tab_sem)
    loads[2].wait()
    for k in range(5):
        want = jnp.int32(0)
        for t in range(2):
            want = jnp.where(route[t, 0] == k, route[t, 1], want)
        rqs[k] = jnp.full((8, TILE), lax.rem(want - e + ne, ne), jnp.int32)
    for c in range(2):
        loads[c].wait()
        pack(raw.at[c], gath.at[c, 0])
    pl.semaphore_wait(barrier, len(others))

    def copy(src, dst, ssem, rsem, to):
        return pltpu.make_async_remote_copy(
            src_ref=src, dst_ref=dst, send_sem=ssem, recv_sem=rsem, device_id=to, device_id_type=MESH
        )

    chunks = [(c, lo, hi) for c in range(2) for lo, hi in CUTS]
    gathers, answers, asks = [], [], []
    for i, (c, lo, hi) in enumerate(chunks):
        at = pl.ds(lo, hi - lo)
        group = [
            copy(gath.at[c, 0, at], gath.at[c, 4 - k, at], xs.at[i, k], xr.at[i, k], to) for k, to in exposures.items()
        ]
        for one in group:
            one.start()
        gathers.append(group)
        if i == 0:
            for d in (-2, -1, 1, 2):
                k = d + CENTRE
                asks.append(copy(rqs.at[k], rqr.at[k], rs.at[k], rr.at[k], along(d)))
                asks[-1].start()

    def chosen(k, c, lo, hi):
        asked = rqr[k, 0:1, :] if k != CENTRE else rqs[k, 0:1, :]
        asked = jnp.broadcast_to(asked, (hi - lo, TILE))
        value = gath[c, 3, lo:hi]
        for j in (2, 1, 0):
            value = jnp.where(asked == j, gath[c, j, lo:hi], value)
        return value

    def answer(i):
        c, lo, hi = chunks[i]
        at = pl.ds(lo, hi - lo)
        for one in gathers[i]:
            one.wait_recv()
        group = []
        for k in (0, 4, 1, 3):
            ysend[c, k, lo:hi] = chosen(k, c, lo, hi)
            group.append(copy(ysend.at[c, k, at], recv[c].at[k, at], ys.at[i, k], yr.at[i, k], along(CENTRE - k)))
            group[-1].start()
        answers.append(group)

    for one in loads[3:] + table_loads:
        one.wait()
    half = len(CUTS)
    last = p >= npatch - 2

    def ready(t, carry):
        prepare(t, route, kc, pick, pick2, deg, rev, term, prow, alpha, square, toep)
        return carry

    @pl.when(jnp.logical_not(last))
    def _():
        lax.fori_loop(0, 2, ready, 0)

    for one in asks:
        one.wait_recv()
    for i in range(half):
        answer(i)

    @pl.when(jnp.logical_not(last))
    def _():
        for t in range(2):
            fill_maps(t, route, alpha, maps)

    for i in range(half, 2 * half):
        answer(i)

    @pl.when(last)
    def _():
        lax.fori_loop(0, 2, ready, 0)
        for t in range(2):
            fill_maps(t, route, alpha, maps)

    for c in range(2):
        recv[c][CENTRE] = chosen(CENTRE, c, 0, PACKED)

    for group in answers[:half]:
        for one in group:
            one.wait_recv()
    fill_lhs([recv_flux[route[t, 0]] for t in range(2)], lhs)
    hbuf[...] = jnp.dot(lhs[...], ca[...], preferred_element_type=F32)
    mix_columns(hbuf, maps, uh, ul)
    z = jnp.dot(rh[...], uh[...], preferred_element_type=F32)
    z = z[0:128] + z[128:256] + jnp.dot(rh[0:128, :], ul[...], preferred_element_type=F32)
    for t in range(2):
        outs[2 * t][...] = sci[0, t] - z[:, t * TILE : (t + 1) * TILE]
    for group in answers[half:]:
        for one in group:
            one.wait_recv()
    fill_lhs([recv_var[route[t, 0]] for t in range(2)], lhs)
    for t in range(2):
        outs[2 * t + 1][...] = sci[1, t] + variance(t, lhs, toep)
    for one in asks + sum(gathers, []) + sum(answers, []):
        one.wait_send()


def per_device(science_flux, science_var, templ_flux, templ_var, kernel_coefs, tile_route):
    hbm = pl.BlockSpec(memory_space=pl.ANY)
    dma = pltpu.SemaphoreType.DMA
    tables = [jnp.asarray(x) for x in make_tables()]
    n = 2 * len(CUTS)
    out = pl.pallas_call(
        difference_kernel,
        out_shape=(jax.ShapeDtypeStruct((TILE, TILE), F32),) * 4,
        in_specs=[hbm] * (6 + N_TABLES),
        out_specs=(pl.BlockSpec(memory_space=pltpu.VMEM),) * 4,
        scratch_shapes=[
            pltpu.VMEM((2, PAD, PAD), F32),
            pltpu.SMEM((2, 5), jnp.int32),
            pltpu.VMEM((kernel_coefs.shape[1], 1, COLS), F32),
            pltpu.VMEM((2, 2, TILE, TILE), F32),
        ]
        + [pltpu.VMEM(x.shape, x.dtype) for x in tables]
        + [
            pltpu.VMEM((2, 4, PACKED, TILE), F32),
            pltpu.VMEM((2, 5, PACKED, TILE), F32),
            pltpu.VMEM((5, PACKED, TILE), F32),
            pltpu.VMEM((5, PACKED, TILE), F32),
            pltpu.VMEM((5, 8, TILE), jnp.int32),
            pltpu.VMEM((5, 8, TILE), jnp.int32),
            pltpu.VMEM((2 * ROWS, 512), BF16),
            pltpu.VMEM((2, 96, 8, TILE), F32),
            pltpu.VMEM((2, 2 * DEGREES, 4, ROWS, TILE), F32),
            pltpu.VMEM((2, 24, TILE), F32),
            pltpu.VMEM((2, 512, 24 * TILE), BF16),
            pltpu.VMEM((2 * ROWS, 1024), F32),
            pltpu.VMEM((2 * DEGREES * ROWS, 256), BF16),
            pltpu.VMEM((2 * DEGREES * ROWS, 256), BF16),
            dma((6,)),
            dma((N_TABLES,)),
            dma((n, 4)),
            dma((n, 4)),
            dma((n, 5)),
            dma((n, 5)),
            dma((5,)),
            dma((5,)),
        ],
        compiler_params=pltpu.CompilerParams(
            collective_id=0, has_side_effects=True, vmem_limit_bytes=VMEM_LIMIT
        ),
        name="difference",
    )(
        templ_flux[0].transpose(1, 0, 2),
        templ_var[0].transpose(1, 0, 2),
        tile_route[0],
        kernel_coefs.transpose(1, 0, 2),
        science_flux[0],
        science_var[0],
        *tables,
    )
    return jnp.stack(out).reshape(1, 2, 2, TILE, TILE)


def solution(mesh):
    return jax.shard_map(
        per_device,
        mesh=mesh,
        in_specs=(
            P("exp", "patch", None, None),
            P("exp", "patch", None, None),
            P("patch", "exp", None, None),
            P("patch", "exp", None, None),
            P("exp", None, None),
            P("exp", "patch", None),
        ),
        out_specs=P("exp", "patch", None, None, None),
        check_vma=False,
    )
```

```python
import jax
import jax.numpy as jnp
import ml_dtypes
import numpy as np
from jax import lax
from jax.experimental import pallas as pl
from jax.experimental.pallas import tpu as pltpu
from jax.sharding import PartitionSpec as P

TILE = 128
HALF = 11
KSIZE = 23
PAD = 150
BASES = 32
TERMS = 6
DET_SIDE = 32
COLS = BASES * TERMS
MAIN = 152
REM = PAD - TILE
PACKED = MAIN + 32
GROUPS = 5
ROWS = 160
CUTS = ((0, 96), (96, PACKED))
N_TABLES = 3
VMEM_LIMIT = 54912 * 2**10
CENTRE = 2
SCALE = TILE * DET_SIDE * 0.5
DEGREES = 6
MESH = pl.DeviceIdType.MESH
BF16 = jnp.bfloat16
F32 = jnp.float32
HIGH = lax.Precision.HIGHEST


def split_np(x):
    hi = x.astype(np.float32).astype(ml_dtypes.bfloat16)
    lo = (x - hi.astype(np.float64)).astype(ml_dtypes.bfloat16)
    return hi, lo


def power_profile(s, m):
    ratio = (np.arange(KSIZE) - HALF) / (1.5 + 1.5 * s)
    return ratio**m * np.exp(-0.5 * ratio * ratio)


def step_up(s, m):
    return (1.5 + 1.5 * s) * np.abs(power_profile(s, m + 1)).sum() / np.abs(power_profile(s, m)).sum()


def banded(profiles):
    out = np.zeros((len(profiles), PAD, TILE))
    for u in range(KSIZE):
        for x in range(TILE):
            out[:, x + u, x] = profiles[:, u]
    return out


def make_tables():
    prof = np.zeros((8, KSIZE))
    wide = np.zeros((2 * DEGREES, KSIZE))
    for s in range(2):
        for m in range(DEGREES):
            row = power_profile(s, m)
            wide[s * DEGREES + m] = row / np.abs(row).sum()
        prof[s * 4 : s * 4 + 4] = wide[s * DEGREES : s * DEGREES + 4]
    toep = banded(prof)
    cols = toep.transpose(1, 0, 2).reshape(PAD, 8 * TILE)
    hi, lo = split_np(cols)
    ca = np.zeros((4 * TILE, 8 * TILE), ml_dtypes.bfloat16)
    ca[0:128] = hi[:128]
    ca[128:256] = hi[:128]
    ca[256:384] = lo[:128]
    ca[384 : 384 + REM] = hi[128:]
    ca[416 : 416 + REM] = hi[128:]
    ca[448 : 448 + REM] = lo[128:]
    rows = np.zeros((TILE, 2 * DEGREES, ROWS))
    rows[:, :, :PAD] = banded(wide).transpose(2, 0, 1)
    hi, lo = split_np(rows.reshape(TILE, 2 * DEGREES * ROWS))
    rh = np.concatenate([hi, lo], 0)
    xdeg = [0, 1, 0, 2, 1, 0]
    ydeg = [0, 0, 1, 0, 1, 2]
    pick = np.zeros((96, COLS), np.float32)
    pick2 = np.zeros((8, COLS), np.float32)
    deg = np.zeros((COLS, TILE), np.float32)
    rev = np.zeros((COLS, TILE), np.float32)
    term = np.zeros((8, COLS), np.float32)
    for b in range(BASES):
        s, mx, my = b % 2, b // 2 % 4, b // 8 % 4
        for k in range(TERMS):
            col = b * TERMS + k
            pick[((s * 4 + mx) * 3 + ydeg[k]) * 4 + my, col] = 1
            pick2[s * 4 + mx, col] = 1
            deg[col] = xdeg[k]
            term[:, col] = k
            for v in range(KSIZE):
                rev[col, -v % TILE] = prof[s * 4 + my, v]
    prow = np.zeros((24, 8), np.float32)
    prow[:KSIZE] = prof.T
    tab = np.zeros((328, 256), np.float32)
    tab[0:96, :COLS] = pick
    tab[96:104, :COLS] = pick2
    tab[104:112, :COLS] = term
    tab[112:304, 0:128] = deg
    tab[112:304, 128:256] = rev
    tab[304:328, 0:8] = prow
    return ca, rh, tab


def fill_lhs(tiles, dst):
    lane = lax.broadcasted_iota(jnp.int32, (32, TILE), 1)
    pieces = []
    for src in tiles:
        main = jnp.concatenate([src[0:MAIN], jnp.zeros((ROWS - MAIN, TILE), F32)], 0)
        hi = main.astype(BF16)
        lo = (main - hi.astype(F32)).astype(BF16)
        other = src[MAIN:PACKED]
        parts = []
        for g in range(GROUPS):
            part = pltpu.roll(other, TILE - REM * g, 1) if g else other
            part = jnp.where(lane < REM, part, 0.0)
            top = part.astype(BF16).astype(F32)
            parts.append((top + pltpu.roll(part - top, 32, 1) + pltpu.roll(top, 64, 1)).astype(BF16))
        pieces.append((hi, lo, jnp.concatenate(parts, 0)))
    for t, (hi, lo, rest) in enumerate(pieces):
        at = slice(t * ROWS, (t + 1) * ROWS)
        dst[at, 0:128] = hi
        dst[at, 128:256] = lo
        dst[at, 256:384] = hi
        dst[at, 384:512] = rest


def prepare(t, route, kc, pick, pick2, deg, rev, term, prow, alpha, square, toep):
    coefs = kc[route[t, 4]]
    row = route[t, 2].astype(F32)
    col = route[t, 3].astype(F32)
    lanes = lax.broadcasted_iota(jnp.int32, (1, TILE), 1).astype(F32)
    xs = (col * TILE + lanes + 0.5) / SCALE - 1.0
    powers = jnp.where(deg[...] == 0.0, 1.0, jnp.where(deg[...] == 1.0, xs, xs * xs))
    rows = jnp.dot(pick[...] * coefs, powers, precision=HIGH, preferred_element_type=F32)
    alpha[t] = jnp.broadcast_to(rows[:, None, :], (96, 8, TILE))
    cx = (col * TILE + TILE * 0.5) / SCALE - 1.0
    cy = (row * TILE + TILE * 0.5) / SCALE - 1.0
    kinds = term[...]
    centre = jnp.where(kinds == 0.0, 1.0, 0.0)
    for k, value in enumerate((cx, cy, cx * cx, cx * cy, cy * cy)):
        centre = jnp.where(kinds == k + 1.0, value, centre)
    mixed = jnp.dot(pick2[...] * centre * coefs, rev[...], precision=HIGH, preferred_element_type=F32)
    kernel = jnp.dot(prow[...], mixed, precision=HIGH, preferred_element_type=F32)
    sub = lax.broadcasted_iota(jnp.int32, (32, TILE), 0)
    lane = lax.broadcasted_iota(jnp.int32, (32, TILE), 1)
    low = lane <= sub
    square[t] = kernel * kernel

    def lag(u, carry):
        at = pl.ds(pl.multiple_of((lax.rem(u, 8) * 3 + lax.div(u, 8)) * TILE, TILE), TILE)
        base = jnp.broadcast_to(square[t, pl.ds(u, 1), :], (TILE, TILE))
        circ = pltpu.roll(base, 0, 1, stride=1, stride_axis=0)
        top = circ[0:32]
        main = jnp.concatenate([jnp.where(low, top, 0.0), circ[32:]], 0)
        rest = jnp.where(low, 0.0, top)
        hi = main.astype(BF16)
        toep[t, 0:128, at] = hi
        toep[t, 128:256, at] = hi
        toep[t, 256:384, at] = (main - hi.astype(F32)).astype(BF16)
        hi = rest.astype(BF16)
        toep[t, 384:416, at] = hi
        toep[t, 416:448, at] = hi
        toep[t, 448:480, at] = (rest - hi.astype(F32)).astype(BF16)
        toep[t, 480:512, at] = jnp.zeros((32, TILE), BF16)
        return carry

    lax.fori_loop(0, KSIZE, lag, 0)


def fill_maps(t, route, alpha, maps):
    subs = lax.broadcasted_iota(jnp.int32, (8, TILE), 0).astype(F32)
    row = route[t, 2].astype(F32) * TILE + (0.5 - HALF)

    def chunk(i, carry):
        yc = (subs + (row + (i * 8).astype(F32))) / SCALE - 1.0
        twice = 2.0 * yc
        at = pl.ds(pl.multiple_of(i * 8, 8), 8)
        for s in range(2):
            for my in range(4):
                abc = [[alpha[t, ((s * 4 + mx) * 3 + j) * 4 + my] for j in range(3)] for mx in range(4)]
                for m in range(DEGREES):
                    total = None
                    if m < 4:
                        a, b, c = abc[m]
                        total = a + yc * (b + yc * c)
                    if 1 <= m <= 4:
                        a, b, c = abc[m - 1]
                        term = (b + twice * c) * np.float32(-step_up(s, m - 1) / SCALE)
                        total = term if total is None else total + term
                    if m >= 2:
                        a, b, c = abc[m - 2]
                        term = c * np.float32(step_up(s, m - 2) * step_up(s, m - 1) / SCALE**2)
                        total = term if total is None else total + term
                    maps[t, s * DEGREES + m, my, at, :] = total
        return carry

    lax.fori_loop(0, ROWS // 8, chunk, 0)


def mix_columns(hbuf, maps, uh, ul):
    def chunk(i, carry):
        at = pl.ds(pl.multiple_of(i * 16, 16), 16)
        for t in range(2):
            here = pl.ds(pl.multiple_of(t * ROWS + i * 16, 16), 16)
            for s in range(2):
                parts = [hbuf[here, (s * 4 + my) * TILE : (s * 4 + my + 1) * TILE] for my in range(4)]
                for m in range(DEGREES):
                    q = s * DEGREES + m
                    total = maps[t, q, 0, at, :] * parts[0]
                    for my in range(1, 4):
                        total = total + maps[t, q, my, at, :] * parts[my]
                    to = pl.ds(pl.multiple_of(q * ROWS + i * 16, 16), 16)
                    cols = slice(t * TILE, (t + 1) * TILE)
                    hi = total.astype(BF16)
                    uh[to, cols] = hi
                    ul[to, cols] = (total - hi.astype(F32)).astype(BF16)
        return carry

    lax.fori_loop(0, ROWS // 16, chunk, 0)


def variance(t, lhs, toep):
    acc = jnp.zeros((TILE, TILE), F32)
    for r in range(0, 8, 2):
        width = 768 if r < 6 else 640
        part = jnp.dot(
            lhs[t * ROWS : (t + 1) * ROWS, :], toep[t, :, r * 384 : r * 384 + width], preferred_element_type=F32
        )
        for k in range(2):
            at = k * 384
            total = part[0:136, at : at + 128] + part[8:144, at + 128 : at + 256]
            if at + 384 <= width:
                total = total + part[16:152, at + 256 : at + 384]
            acc = acc + total[r + k : r + k + TILE]
    return acc


def fetch(refs, buffers, sem):
    copies = [pltpu.make_async_copy(src, dst, sem.at[i]) for i, (src, dst) in enumerate(zip(refs, buffers))]
    for one in copies:
        one.start()
    return copies


def pack(raw, dst):
    dst[0:PAD, :] = raw[:, 0:TILE]
    dst[PAD:MAIN, :] = jnp.zeros((MAIN - PAD, TILE), F32)
    packed = jnp.zeros((32, TILE), F32)
    for g in range(GROUPS):
        n = min(32, PAD - 32 * g)
        part = raw[32 * g : 32 * g + n, TILE:PAD]
        part = jnp.concatenate([part, jnp.zeros((n, TILE - REM), F32)], 1)
        if n < 32:
            part = jnp.concatenate([part, jnp.zeros((32 - n, TILE), F32)], 0)
        if g:
            part = pltpu.roll(part, REM * g, 1)
        packed = packed + part
    dst[MAIN:PACKED, :] = packed


def difference_kernel(*refs):
    n = N_TABLES
    tf, tv, route, kc_in, sf_in, sv_in = refs[:6]
    tables_in, outs = refs[6 : 6 + n], refs[6 + n : 10 + n]
    raw, kc, sci = refs[10 + n : 13 + n]
    tables = refs[13 + n : 13 + 2 * n]
    gath, ysend, recv_flux, recv_var, rqs, rqr, lhs, alpha, maps, square, toep, hbuf, uh, ul = refs[13 + 2 * n : 27 + 2 * n]
    ld_sem, tab_sem, xs, xr, ys, yr, rs, rr = refs[27 + 2 * n :]
    recv = (recv_flux, recv_var)
    ca, rh, tab = tables
    pick, pick2, term = (tab.at[lo:hi, 0:COLS] for lo, hi in ((0, 96), (96, 104), (104, 112)))
    deg, rev = tab.at[112:304, 0:128], tab.at[112:304, 128:256]
    prow = tab.at[304:328, 0:8]

    e = lax.axis_index("exp")
    p = lax.axis_index("patch")
    ne = lax.axis_size("exp")
    npatch = lax.axis_size("patch")
    exposures = {k: (lax.rem(e + k, ne), p) for k in (2, 1, 3)}

    def along(d):
        return (e, lax.rem(p + d + npatch, npatch))

    barrier = pltpu.get_barrier_semaphore()
    others = list(exposures.values()) + [along(d) for d in (-2, -1, 1, 2)]
    for other in others:
        pl.semaphore_signal(barrier, inc=1, device_id=other, device_id_type=MESH)
    loads = fetch(
        (tf.at[:, 0, :], tv.at[:, 0, :], kc_in, sf_in, sv_in),
        (raw.at[0], raw.at[1], kc, sci.at[0], sci.at[1]),
        ld_sem,
    )
    table_loads = fetch(tables_in, tables, tab_sem)
    for k in range(5):
        want = jnp.int32(0)
        for t in range(2):
            want = jnp.where(route[t, 0] == k, route[t, 1], want)
        rqs[k] = jnp.full((8, TILE), lax.rem(want - e + ne, ne), jnp.int32)
    for c in range(2):
        loads[c].wait()
        pack(raw.at[c], gath.at[c, 0])
    pl.semaphore_wait(barrier, len(others))

    def copy(src, dst, ssem, rsem, to):
        return pltpu.make_async_remote_copy(
            src_ref=src, dst_ref=dst, send_sem=ssem, recv_sem=rsem, device_id=to, device_id_type=MESH
        )

    chunks = [(c, lo, hi) for c in range(2) for lo, hi in CUTS]
    gathers, answers, asks = [], [], []
    for i, (c, lo, hi) in enumerate(chunks):
        at = pl.ds(lo, hi - lo)
        group = [
            copy(gath.at[c, 0, at], gath.at[c, 4 - k, at], xs.at[i, k], xr.at[i, k], to) for k, to in exposures.items()
        ]
        for one in group:
            one.start()
        gathers.append(group)
        if i == 0:
            for d in (-2, -1, 1, 2):
                k = d + CENTRE
                asks.append(copy(rqs.at[k], rqr.at[k], rs.at[k], rr.at[k], along(d)))
                asks[-1].start()

    def chosen(k, c, lo, hi):
        asked = rqr[k, 0:1, :] if k != CENTRE else rqs[k, 0:1, :]
        asked = jnp.broadcast_to(asked, (hi - lo, TILE))
        value = gath[c, 3, lo:hi]
        for j in (2, 1, 0):
            value = jnp.where(asked == j, gath[c, j, lo:hi], value)
        return value

    def answer(i):
        c, lo, hi = chunks[i]
        at = pl.ds(lo, hi - lo)
        for one in gathers[i]:
            one.wait_recv()
        group = []
        for k in (0, 4, 1, 3):
            ysend[c, k, lo:hi] = chosen(k, c, lo, hi)
            group.append(copy(ysend.at[c, k, at], recv[c].at[k, at], ys.at[i, k], yr.at[i, k], along(CENTRE - k)))
            group[-1].start()
        answers.append(group)

    for one in loads[2:] + table_loads:
        one.wait()
    half = len(CUTS)
    last = p >= npatch - 2

    def ready(t, carry):
        prepare(t, route, kc, pick, pick2, deg, rev, term, prow, alpha, square, toep)
        return carry

    @pl.when(jnp.logical_not(last))
    def _():
        lax.fori_loop(0, 2, ready, 0)

    for one in asks:
        one.wait_recv()
    for i in range(half):
        answer(i)

    @pl.when(jnp.logical_not(last))
    def _():
        for t in range(2):
            fill_maps(t, route, alpha, maps)

    for i in range(half, 2 * half):
        answer(i)

    @pl.when(last)
    def _():
        lax.fori_loop(0, 2, ready, 0)
        for t in range(2):
            fill_maps(t, route, alpha, maps)

    for c in range(2):
        recv[c][CENTRE] = chosen(CENTRE, c, 0, PACKED)

    for group in answers[:half]:
        for one in group:
            one.wait_recv()
    fill_lhs([recv_flux[route[t, 0]] for t in range(2)], lhs)
    hbuf[...] = jnp.dot(lhs[...], ca[...], preferred_element_type=F32)
    mix_columns(hbuf, maps, uh, ul)
    z = jnp.dot(rh[...], uh[...], preferred_element_type=F32)
    z = z[0:128] + z[128:256] + jnp.dot(rh[0:128, :], ul[...], preferred_element_type=F32)
    for t in range(2):
        outs[2 * t][...] = sci[0, t] - z[:, t * TILE : (t + 1) * TILE]
    for group in answers[half:]:
        for one in group:
            one.wait_recv()
    fill_lhs([recv_var[route[t, 0]] for t in range(2)], lhs)
    for t in range(2):
        outs[2 * t + 1][...] = sci[1, t] + variance(t, lhs, toep)
    for one in asks + sum(gathers, []) + sum(answers, []):
        one.wait_send()


def per_device(science_flux, science_var, templ_flux, templ_var, kernel_coefs, tile_route):
    hbm = pl.BlockSpec(memory_space=pl.ANY)
    dma = pltpu.SemaphoreType.DMA
    tables = [jnp.asarray(x) for x in make_tables()]
    n = 2 * len(CUTS)
    out = pl.pallas_call(
        difference_kernel,
        out_shape=(jax.ShapeDtypeStruct((TILE, TILE), F32),) * 4,
        in_specs=[hbm, hbm, pl.BlockSpec(memory_space=pltpu.SMEM)] + [hbm] * (3 + N_TABLES),
        out_specs=(pl.BlockSpec(memory_space=pltpu.VMEM),) * 4,
        scratch_shapes=[
            pltpu.VMEM((2, PAD, PAD), F32),
            pltpu.VMEM((kernel_coefs.shape[1], 1, COLS), F32),
            pltpu.VMEM((2, 2, TILE, TILE), F32),
        ]
        + [pltpu.VMEM(x.shape, x.dtype) for x in tables]
        + [
            pltpu.VMEM((2, 4, PACKED, TILE), F32),
            pltpu.VMEM((2, 5, PACKED, TILE), F32),
            pltpu.VMEM((5, PACKED, TILE), F32),
            pltpu.VMEM((5, PACKED, TILE), F32),
            pltpu.VMEM((5, 8, TILE), jnp.int32),
            pltpu.VMEM((5, 8, TILE), jnp.int32),
            pltpu.VMEM((2 * ROWS, 512), BF16),
            pltpu.VMEM((2, 96, 8, TILE), F32),
            pltpu.VMEM((2, 2 * DEGREES, 4, ROWS, TILE), F32),
            pltpu.VMEM((2, 24, TILE), F32),
            pltpu.VMEM((2, 512, 24 * TILE), BF16),
            pltpu.VMEM((2 * ROWS, 1024), F32),
            pltpu.VMEM((2 * DEGREES * ROWS, 256), BF16),
            pltpu.VMEM((2 * DEGREES * ROWS, 256), BF16),
            dma((5,)),
            dma((N_TABLES,)),
            dma((n, 4)),
            dma((n, 4)),
            dma((n, 5)),
            dma((n, 5)),
            dma((5,)),
            dma((5,)),
        ],
        compiler_params=pltpu.CompilerParams(
            collective_id=0, has_side_effects=True, vmem_limit_bytes=VMEM_LIMIT
        ),
        name="difference",
    )(
        templ_flux[0].transpose(1, 0, 2),
        templ_var[0].transpose(1, 0, 2),
        tile_route[0],
        kernel_coefs.transpose(1, 0, 2),
        science_flux[0],
        science_var[0],
        *tables,
    )
    return jnp.stack(out).reshape(1, 2, 2, TILE, TILE)


def solution(mesh):
    return jax.shard_map(
        per_device,
        mesh=mesh,
        in_specs=(
            P("exp", "patch", None, None),
            P("exp", "patch", None, None),
            P("patch", "exp", None, None),
            P("patch", "exp", None, None),
            P("exp", None, None),
            P("exp", "patch", None),
        ),
        out_specs=P("exp", "patch", None, None, None),
        check_vma=False,
    )
```
